32 devices in a mesh: dom: 16 (over z, y, core), orient: 2 (over x).
Axes of the slice: x: 2, y: 2, z: 4, core: 2. Of those that a mesh axis runs over, the one named last changes fastest.
Arguments:
- particles: bfloat16 [256, 64, 128], P(('dom', 'orient')), may hold values from -48 to 48
- slices: bfloat16 [16, 64, 128], P('orient'), may hold values from -5 to 5
- freq_mask: int32 [64, 64], replicated, may hold values 0 or 1
- slice_class: int32 [16], replicated, may hold values from 0 to 7
- slice_orient: int32 [16], replicated, may hold values from 0 to 31
- class_prior: float32 [8], replicated, may hold values from -1 to 1
- orient_prior: float32 [32], replicated, may hold values from -1 to 1
Outputs:
- back_proj: float32 [16, 64, 128], P('orient', 'dom')
- occupancy: float32 [16], P('orient')
- loglik: float32 [256], P(('dom', 'orient'))
The draws below stay inside these ranges and needn't reach their ends.
All inputs are finite; a program needn't handle non-finite values.
Results may differ from the reference program's by a relative error of at most 0.0034.
Values may be sent and summed in bfloat16 or wider, within the bound.
No kernel may reach another device: no remote copies, remote signals or barrier semaphores. Data moves between devices by JAX's collectives and lax.ppermute only.
A program may use at most 128 MiB of HBM per device.

```python
import math
import jax
import jax.numpy as jnp
from jax import lax

CROP = 64
TS = 16
CLASSES = 8
ORI_BINS = 32
P_SIZE = 256
NSL = 16


def slice_base(key):
    return jnp.clip(jax.random.normal(key, (NSL, CROP, 2 * CROP), jnp.float32), -5.0, 5.0)


def draw_slices(key, part):
    base = slice_base(key)
    return base.astype(jnp.bfloat16)


def draw_particles(key, part):
    base = slice_base(key)
    key = jax.random.fold_in(key, 7)
    pick_key, noise_key = jax.random.split(key, 2)
    chosen = jax.random.randint(pick_key, (P_SIZE,), 0, NSL)
    noise = jax.random.normal(noise_key, (P_SIZE, CROP, 2 * CROP), jnp.float32)
    signal = 0.08 * base[chosen]
    return (signal + noise).astype(jnp.bfloat16)


def touch_ends(values, stream_key, least, high):
    extent = values.shape
    index_at = [jax.random.randint(jax.random.fold_in(stream_key, axis), (), 0, extent[axis]) for axis in range(len(extent))]
    values = values.at[tuple(index_at)].set(least)
    longest = extent.index(max(extent))
    index_at[longest] = (index_at[longest] + 1) % extent[longest]
    return values.at[tuple(index_at)].set(high)


def setup_inputs(seed: int = 0) -> dict:
    splits = jax.random.split(jax.random.key(seed), 8)
    return {
        "particles": draw_particles(jax.random.fold_in(splits[7], 71), 0),
        "slices": draw_slices(jax.random.fold_in(splits[7], 71), 0),
        "freq_mask": touch_ends((jax.random.randint(splits[2], (CROP, CROP), 0, 4) < 3).astype(jnp.int32), jax.random.fold_in(splits[2], 1), 0, 1),
        "slice_class": touch_ends(jax.random.randint(splits[3], (NSL,), 0, CLASSES), jax.random.fold_in(splits[3], 1), 0, CLASSES - 1).astype(jnp.int32),
        "slice_orient": touch_ends(jax.random.randint(splits[4], (NSL,), 0, ORI_BINS), jax.random.fold_in(splits[4], 1), 0, ORI_BINS - 1).astype(jnp.int32),
        "class_prior": jnp.clip(jax.random.uniform(splits[5], (CLASSES,), jnp.float32, -1.0, 1.0), -1.0, 1.0),
        "orient_prior": jnp.clip(jax.random.uniform(splits[6], (ORI_BINS,), jnp.float32, -1.0, 1.0), -1.0, 1.0),
    }


HIGH = lax.Precision.HIGHEST


def phase_tables(crop, shifts):
    freq = jnp.arange(crop, dtype=jnp.float32) - crop // 2
    offset = jnp.arange(shifts, dtype=jnp.float32) - shifts // 2
    angle = (2.0 * math.pi / crop) * freq[:, None] * offset[None, :]
    return jnp.cos(angle), jnp.sin(angle)


def score_table(cosine, sine):
    upper = jnp.concatenate([cosine, sine], axis=1)
    lower = jnp.concatenate([-sine, cosine], axis=1)
    return jnp.concatenate([upper, lower], axis=0).astype(jnp.bfloat16)


def spread_table(cosine, sine):
    return jnp.concatenate([cosine.T, -sine.T], axis=1).astype(jnp.bfloat16)


def slice_prior(slice_class, slice_orient, class_prior, orient_prior):
    class_hot = (slice_class[:, None] == jnp.arange(class_prior.shape[0], dtype=jnp.int32)[None, :]).astype(class_prior.dtype)
    orient_hot = (slice_orient[:, None] == jnp.arange(orient_prior.shape[0], dtype=jnp.int32)[None, :]).astype(orient_prior.dtype)
    return jnp.sum(class_hot * class_prior[None, :], axis=1) + jnp.sum(orient_hot * orient_prior[None, :], axis=1)


def score_block(parts, block, weight_mask, forward, cosine, sine, prior):
    half = parts.shape[-1] // 2
    x_re = parts[..., :half].astype(jnp.float32)[:, None]
    x_im = parts[..., half:].astype(jnp.float32)[:, None]
    s_re = block[..., :half].astype(jnp.float32)[None]
    s_im = block[..., half:].astype(jnp.float32)[None]
    cross_re = (x_re * s_re + x_im * s_im) * weight_mask
    cross_im = (x_im * s_re - x_re * s_im) * weight_mask
    cross = jnp.concatenate([cross_re, cross_im], axis=-1).astype(jnp.bfloat16)
    rowcorr = jnp.einsum('abyk,kt->abyt', cross.astype(jnp.float32), forward.astype(jnp.float32), precision=HIGH)
    shifts = cosine.shape[1]
    corr = jnp.einsum('yu,abyt->abut', cosine, rowcorr[..., :shifts], precision=HIGH) - jnp.einsum('yu,abyt->abut', sine, rowcorr[..., shifts:], precision=HIGH)
    power = jnp.sum((s_re * s_re + s_im * s_im) * weight_mask, axis=(2, 3))
    crop = weight_mask.shape[0]
    return (corr - 0.5 * power[:, :, None, None]) / crop + prior[None, :, None, None]


def back_block(parts, weights, weight_mask, spread, cosine, sine):
    half = parts.shape[-1] // 2
    spread_x = jnp.einsum('abuv,vk->abuk', weights.astype(jnp.float32), spread.astype(jnp.float32), precision=HIGH)
    a_re = spread_x[..., :half]
    a_im = spread_x[..., half:]
    g_re = jnp.einsum('yu,abuk->abyk', cosine, a_re, precision=HIGH) + jnp.einsum('yu,abuk->abyk', sine, a_im, precision=HIGH)
    g_im = jnp.einsum('yu,abuk->abyk', cosine, a_im, precision=HIGH) - jnp.einsum('yu,abuk->abyk', sine, a_re, precision=HIGH)
    x_re = parts[..., :half].astype(jnp.float32)[:, None]
    x_im = parts[..., half:].astype(jnp.float32)[:, None]
    b_re = jnp.sum(g_re * x_re - g_im * x_im, axis=0) * weight_mask
    b_im = jnp.sum(g_re * x_im + g_im * x_re, axis=0) * weight_mask
    return jnp.concatenate([b_re, b_im], axis=-1)


def reference(particles, slices, freq_mask, slice_class, slice_orient, class_prior, orient_prior):
    crop = slices.shape[1]
    cosine, sine = phase_tables(crop, TS)
    forward = score_table(cosine, sine)
    spread = spread_table(cosine, sine)
    weight_mask = freq_mask.astype(jnp.float32)
    prior = slice_prior(slice_class, slice_orient, class_prior, orient_prior)

    def one_particle(carry, part):
        image, occupancy = carry
        parts = part[None]
        logits = score_block(parts, slices, weight_mask, forward, cosine, sine, prior)[0]
        top = jnp.max(logits)
        total = top + jnp.log(jnp.sum(jnp.exp(logits - top)))
        weights = jnp.exp(logits - total).astype(jnp.bfloat16)
        image = image + back_block(parts, weights[None], weight_mask, spread, cosine, sine)
        occupancy = occupancy + jnp.sum(weights.astype(jnp.float32), axis=(1, 2))
        return (image, occupancy), total

    start = (jnp.zeros(slices.shape, jnp.float32), jnp.zeros((slices.shape[0],), jnp.float32))
    (image, occupancy), loglik = lax.scan(one_particle, start, particles)
    return image, occupancy, loglik
```

```python
import functools
import math

import jax
import jax.numpy as jnp
import ml_dtypes
import numpy as np
from jax import lax
from jax.experimental import pallas as pl
from jax.experimental.pallas import tpu as pltpu
from jax.sharding import PartitionSpec as P

TS = 16
F32 = jnp.float32
BF16 = jnp.bfloat16
VMEM_LIMIT = 24 * 1024 * 1024


def phase_tables(crop):
    freq = np.arange(crop, dtype=np.float64) - crop // 2
    offset = np.arange(TS, dtype=np.float64) - TS // 2
    angle = 2.0 * math.pi / crop * freq[:, None] * offset[None, :]
    return np.cos(angle).astype(np.float32), np.sin(angle).astype(np.float32)


def high_low(table):
    high = table.astype(ml_dtypes.bfloat16)
    low = (table - high.astype(np.float32)).astype(ml_dtypes.bfloat16)
    return high, low


def score_tables(crop, share):
    cosine, sine = phase_tables(crop)
    rows = np.zeros((share, 2, crop, 2, share, TS), np.float32)
    for j in range(share):
        rows[j, 0, :, 0, j] = cosine
        rows[j, 0, :, 1, j] = sine
        rows[j, 1, :, 0, j] = -sine
        rows[j, 1, :, 1, j] = cosine
    rows = rows.reshape(share * 2 * crop, 2 * share * TS).astype(ml_dtypes.bfloat16)
    high, low = high_low(np.concatenate([cosine.T, -sine.T], axis=1))
    columns = np.concatenate(
        [np.concatenate([high, high], axis=1), np.concatenate([low, np.zeros_like(low)], axis=1)], axis=0
    )
    return rows, columns


def back_tables(crop, share, order):
    cosine, sine = phase_tables(crop)
    rows = np.zeros((share, TS, 2, share, 2, crop), np.float32)
    for place, j in enumerate(order):
        rows[j, :, 0, place, 0] = cosine.T
        rows[j, :, 0, place, 1] = -sine.T
        rows[j, :, 1, place, 0] = -sine.T
        rows[j, :, 1, place, 1] = -cosine.T
    rows = rows.reshape(share * TS, 2 * share * 2 * crop).astype(ml_dtypes.bfloat16)
    high, low = high_low(np.concatenate([cosine, sine], axis=1))
    return rows, np.concatenate([high, high, low], axis=1)


def both_halves(mask_ref):
    mask = mask_ref[...].astype(F32)
    return jnp.concatenate([mask, mask], axis=1)


def score_kernel(
    share,
    own_ref,
    class_ref,
    orient_ref,
    class_prior_ref,
    orient_prior_ref,
    x_ref,
    s_ref,
    mask_ref,
    rows_ref,
    columns_ref,
    logits_ref,
    lse_ref,
    cross,
    first,
    second,
    plain,
    swapped,
):
    count, crop, width = x_ref.shape
    half = width // 2
    mask = both_halves(mask_ref)
    left = lax.broadcasted_iota(jnp.int32, (crop, width), 1) < half
    slot = lax.broadcasted_iota(jnp.int32, (1, share * TS), 1) // TS
    bias = jnp.zeros((1, share * TS), F32)
    start = own_ref[0] * share
    for j in range(share):
        s = s_ref[j].astype(F32) * mask
        turned = pltpu.roll(s, half, 1)
        first[j] = jnp.where(left, s, turned)
        second[j] = jnp.where(left, turned, -s)
        power = jnp.sum(s * s)
        prior = class_prior_ref[class_ref[start + j]] + orient_prior_ref[orient_ref[start + j]]
        bias = jnp.where(slot == j, prior - power * (0.5 / crop), bias)
    for i in range(count):
        x = x_ref[i].astype(F32)
        plain[i] = x
        swapped[i] = pltpu.roll(x, half, 1)
    for at in range(0, crop, 16):
        for j in range(share):
            a, b = first[j, at : at + 16], second[j, at : at + 16]
            for i in range(count):
                value = plain[i, at : at + 16] * a + swapped[i, at : at + 16] * b
                cross[i * crop + at : i * crop + at + 16, j * width : (j + 1) * width] = value.astype(BF16)
    rowcorr = jnp.dot(cross[...], rows_ref[...], preferred_element_type=F32)
    high = rowcorr.astype(BF16)
    low = (rowcorr - high.astype(F32)).astype(BF16)
    lanes = share * TS
    stacked = jnp.concatenate(
        [
            jnp.concatenate(
                [part[i * crop : (i + 1) * crop, k * lanes : (k + 1) * lanes] for part in (high, low) for k in (0, 1)],
                axis=0,
            )
            for i in range(count)
        ],
        axis=1,
    )
    corr = jnp.dot(columns_ref[...], stacked, preferred_element_type=F32)
    corr = (corr[:TS] + corr[TS:]) * (1.0 / crop)
    for i in range(count):
        logits = corr[:, i * lanes : (i + 1) * lanes] + bias
        logits_ref[i] = logits
        top = jnp.max(logits, keepdims=True)
        total = jnp.sum(jnp.exp(logits - top), keepdims=True)
        lse_ref[i : i + 1, :] = jnp.broadcast_to(top + jnp.log(total), (1, lse_ref.shape[1]))


def back_kernel(n, share, pack, *refs):
    logits_refs, x_refs = refs[:n], refs[n : 2 * n]
    lse_ref, mask_ref, rows_ref, columns_ref, out_ref, mass_ref, doubled_re, doubled_im, high, low = refs[2 * n :]
    count, crop, width = x_refs[0].shape
    half = width // 2
    left = lax.broadcasted_iota(jnp.int32, (crop, width), 1) < half
    sign = jnp.where(left[:1], -1.0, 1.0)
    mask = both_halves(mask_ref)
    mass = jnp.zeros((1, share * TS), F32)
    for r in range(n):
        weights = []
        for i in range(count):
            k = r * count + i
            weight = jnp.exp(logits_refs[r][i] - lse_ref[k : k + 1, :]).astype(BF16)
            mass = mass + jnp.sum(weight.astype(F32), axis=0, keepdims=True)
            weights.append(weight)
            x = x_refs[r][i].astype(F32)
            turned = pltpu.roll(x, half, 1)
            doubled_re[k] = jnp.where(left, x, turned)
            doubled_im[k] = jnp.where(left, turned, x)
        spread = jnp.dot(jnp.concatenate(weights, axis=0), rows_ref[...], preferred_element_type=F32)
        rounded = spread.astype(BF16)
        span = slice(r * count * TS, (r + 1) * count * TS)
        high[span] = rounded
        low[span] = (spread - rounded.astype(F32)).astype(BF16)
    mass_ref[...] = jnp.broadcast_to(mass, mass_ref.shape)
    forms = share * width
    wide = pack * width
    columns = columns_ref[...]
    for group in range(share // pack):
        re = jnp.zeros((crop, wide), F32)
        im = jnp.zeros((crop, wide), F32)
        for k in range(n * count):
            rows = slice(k * TS, (k + 1) * TS)
            here = slice(group * wide, (group + 1) * wide)
            there = slice(forms + group * wide, forms + (group + 1) * wide)
            a, b = high[rows, here], high[rows, there]
            terms = jnp.concatenate([a, b, low[rows, here], low[rows, there], a, b], axis=0)
            kernel = jnp.dot(columns, terms, preferred_element_type=F32)
            x_re, x_im = doubled_re[k], doubled_im[k]
            re = re + kernel * jnp.concatenate([x_re] * pack, axis=1)
            im = im + kernel * jnp.concatenate([x_im] * pack, axis=1)
        images = []
        for p in range(pack):
            here = slice(p * width, (p + 1) * width)
            images.append((re[:, here] + pltpu.roll(im[:, here], half, 1) * sign) * mask)
        block = 8 // pack
        for tile in range(crop // 8):
            for b in range(pack):
                rows = slice(tile * 8 + b * block, tile * 8 + (b + 1) * block)
                out_ref[tile * pack + b, group] = jnp.concatenate([image[rows] for image in images], axis=0)


def log_add(a, b):
    top = jnp.maximum(a, b)
    return top + jnp.log(jnp.exp(a - top) + jnp.exp(b - top))


def bits(count):
    return count.bit_length() - 1


def shards(n_dom, n_orient, particles, slices, freq_mask, slice_class, slice_orient, class_prior, orient_prior):
    count, crop, width = particles.shape
    share = slices.shape[0]
    lanes = share * TS
    block = crop // n_dom
    pack = 8 // block
    smem = pl.BlockSpec(memory_space=pltpu.SMEM)
    vmem = pl.BlockSpec(memory_space=pltpu.VMEM)
    own = lax.axis_index("orient")
    me = lax.axis_index("dom")
    score_rows, score_columns = score_tables(crop, share)
    groups = share // pack
    order = [p * groups + g for g in range(groups) for p in range(pack)]
    back_rows, back_columns = back_tables(crop, share, order)

    def swap(value, axis, size, step):
        return lax.ppermute(value, axis, [(i, i ^ step) for i in range(size)])

    flops = 2 * count * crop * share * width * 2 * lanes
    score = pl.pallas_call(
        functools.partial(score_kernel, share),
        out_shape=(
            jax.ShapeDtypeStruct((count, TS, lanes), F32),
            jax.ShapeDtypeStruct((count, 128), F32),
        ),
        in_specs=[smem] * 5 + [vmem] * 5,
        out_specs=(vmem, vmem),
        scratch_shapes=[
            pltpu.VMEM((count * crop, share * width), BF16),
            pltpu.VMEM((share, crop, width), F32),
            pltpu.VMEM((share, crop, width), F32),
            pltpu.VMEM((count, crop, width), F32),
            pltpu.VMEM((count, crop, width), F32),
        ],
        compiler_params=pltpu.CompilerParams(vmem_limit_bytes=VMEM_LIMIT),
        cost_estimate=pl.CostEstimate(flops=flops, bytes_accessed=1 << 20, transcendentals=count * TS * lanes),
        name="score",
    )

    def scores(parts):
        return score(
            own[None].astype(jnp.int32), slice_class, slice_orient, class_prior, orient_prior,
            parts, slices, freq_mask, jnp.asarray(score_rows), jnp.asarray(score_columns),
        )

    slots = [particles] + [swap(particles, "orient", n_orient, r) for r in range(1, n_orient)]
    scored = [scores(parts) for parts in slots]
    lse = jnp.stack([s[1] for s in scored])
    for b in range(bits(n_orient)):
        theirs = swap(lse, "orient", n_orient, 1 << b)
        lse = log_add(lse, jnp.stack([theirs[r ^ (1 << b)] for r in range(n_orient)]))
    loglik = lse[0, :, 0]

    total = n_orient * count
    terms, mass = pl.pallas_call(
        functools.partial(back_kernel, n_orient, share, pack),
        out_shape=(
            jax.ShapeDtypeStruct((n_dom, groups, 8, width), F32),
            jax.ShapeDtypeStruct((8, lanes), F32),
        ),
        in_specs=[vmem] * (2 * n_orient + 4),
        out_specs=(vmem, vmem),
        scratch_shapes=[
            pltpu.VMEM((total, crop, width), F32),
            pltpu.VMEM((total, crop, width), F32),
            pltpu.VMEM((total * TS, 2 * share * width), BF16),
            pltpu.VMEM((total * TS, 2 * share * width), BF16),
        ],
        compiler_params=pltpu.CompilerParams(vmem_limit_bytes=VMEM_LIMIT),
        name="back",
    )(
        *[s[0] for s in scored], *slots, lse.reshape(total, 128), freq_mask,
        jnp.asarray(back_rows), jnp.asarray(back_columns),
    )

    mass = jnp.sum(mass[0].reshape(share, TS), axis=1)
    mass = jnp.pad(mass[None, :], ((0, 0), (0, 128 - share)))
    for b in range(bits(n_dom)):
        halves = terms.reshape(terms.shape[0] // 2, 2, *terms.shape[1:])
        bit = (me >> b) & 1
        keep = lax.dynamic_index_in_dim(halves, bit, 1, keepdims=False)
        send = lax.dynamic_index_in_dim(halves, 1 - bit, 1, keepdims=False).astype(BF16)
        high = mass.astype(BF16)
        middle = (mass - high.astype(F32)).astype(BF16)
        low = (mass - high.astype(F32) - middle.astype(F32)).astype(BF16)
        tail = jnp.concatenate([high, middle, low, jnp.zeros((13, 128), BF16)], axis=0).reshape(2, 8, 128)
        got = swap(jnp.concatenate([send.reshape(-1, 8, width), tail], axis=0), "dom", n_dom, 1 << b).astype(F32)
        terms = keep + got[:-2].reshape(keep.shape)
        mass = mass + got[-2, 0:1] + got[-2, 1:2] + got[-2, 2:3]
    image = terms[0].reshape(groups, pack, block, width).transpose(1, 0, 2, 3).reshape(share, block, width)
    return image, mass[0, :share], loglik


def solution(mesh):
    placed = (P(("dom", "orient"), None, None), P("orient", None, None), P(), P(), P(), P(), P())
    return jax.shard_map(
        functools.partial(shards, mesh.shape["dom"], mesh.shape["orient"]),
        mesh=mesh,
        in_specs=placed,
        out_specs=(P("orient", "dom", None), P("orient"), P(("dom", "orient"))),
        check_vma=False,
    )
```

```python
import functools
import math

import jax
import jax.numpy as jnp
import ml_dtypes
import numpy as np
from jax import lax
from jax.experimental import pallas as pl
from jax.experimental.pallas import tpu as pltpu
from jax.sharding import PartitionSpec as P

TS = 16
F32 = jnp.float32
BF16 = jnp.bfloat16
VMEM_LIMIT = 24 * 1024 * 1024


def phase_tables(crop):
    freq = np.arange(crop, dtype=np.float64) - crop // 2
    offset = np.arange(TS, dtype=np.float64) - TS // 2
    angle = 2.0 * math.pi / crop * freq[:, None] * offset[None, :]
    return np.cos(angle).astype(np.float32), np.sin(angle).astype(np.float32)


def high_low(table):
    high = table.astype(ml_dtypes.bfloat16)
    low = (table - high.astype(np.float32)).astype(ml_dtypes.bfloat16)
    return high, low


def score_tables(crop, share):
    cosine, sine = phase_tables(crop)
    rows = np.zeros((share, 2, crop, 2, share, TS), np.float32)
    for j in range(share):
        rows[j, 0, :, 0, j] = cosine
        rows[j, 0, :, 1, j] = sine
        rows[j, 1, :, 0, j] = -sine
        rows[j, 1, :, 1, j] = cosine
    rows = rows.reshape(share * 2 * crop, 2 * share * TS).astype(ml_dtypes.bfloat16)
    high, low = high_low(np.concatenate([cosine.T, -sine.T], axis=1))
    columns = np.concatenate(
        [np.concatenate([high, high], axis=1), np.concatenate([low, np.zeros_like(low)], axis=1)], axis=0
    )
    return rows, columns


def back_tables(crop, share, order):
    cosine, sine = phase_tables(crop)
    rows = np.zeros((share, TS, 2, share, 2, crop), np.float32)
    for place, j in enumerate(order):
        rows[j, :, 0, place, 0] = cosine.T
        rows[j, :, 0, place, 1] = -sine.T
        rows[j, :, 1, place, 0] = -sine.T
        rows[j, :, 1, place, 1] = -cosine.T
    rows = rows.reshape(share * TS, 2 * share * 2 * crop).astype(ml_dtypes.bfloat16)
    high, low = high_low(np.concatenate([cosine, sine], axis=1))
    return rows, np.concatenate([high, high, low], axis=1)


def score_block(plain, swapped, first_ref, second_ref, bias, rows_ref, columns_ref, cross, logits_ref, lse_ref):
    count, crop, width = plain.shape
    share = first_ref.shape[0]
    lanes = share * TS
    for at in range(0, crop, 16):
        for j in range(share):
            a, b = first_ref[j, at : at + 16], second_ref[j, at : at + 16]
            for i in range(count):
                value = plain[i, at : at + 16] * a + swapped[i, at : at + 16] * b
                cross[i * crop + at : i * crop + at + 16, j * width : (j + 1) * width] = value.astype(BF16)
    rowcorr = jnp.dot(cross[...], rows_ref[...], preferred_element_type=F32)
    high = rowcorr.astype(BF16)
    low = (rowcorr - high.astype(F32)).astype(BF16)
    stacked = jnp.concatenate(
        [
            jnp.concatenate(
                [part[i * crop : (i + 1) * crop, k * lanes : (k + 1) * lanes] for part in (high, low) for k in (0, 1)],
                axis=0,
            )
            for i in range(count)
        ],
        axis=1,
    )
    corr = jnp.dot(columns_ref[...], stacked, preferred_element_type=F32)
    corr = (corr[:TS] + corr[TS:]) * (1.0 / crop)
    logits = [corr[:, i * lanes : (i + 1) * lanes] + bias for i in range(count)]
    for i in range(count):
        logits_ref[i] = logits[i]
    tops = jnp.concatenate([jnp.max(value, axis=0, keepdims=True) for value in logits], axis=0)
    top = jnp.max(tops, axis=1, keepdims=True)
    sums = [jnp.sum(jnp.exp(logits[i] - top[i : i + 1]), axis=0, keepdims=True) for i in range(count)]
    total = jnp.sum(jnp.concatenate(sums, axis=0), axis=1, keepdims=True)
    lse_ref[...] = jnp.broadcast_to(top + jnp.log(total), lse_ref.shape)


def split_particles(x_ref, plain, swapped):
    for i in range(x_ref.shape[0]):
        x = x_ref[i].astype(F32)
        plain[i] = x
        swapped[i] = pltpu.roll(x, x.shape[1] // 2, 1)


def first_kernel(*refs):
    sources, (logits_ref, lse_ref, first, second, bias_ref), kept = refs[:11], refs[11:16], refs[16:22]
    s_ref, class_ref, orient_ref, class_prior_ref, orient_prior_ref, cross, plain, swapped, sems = refs[22:]
    x_ref, mask_ref, rows_ref, columns_ref, back_rows_ref, back_columns_ref = kept
    targets = (
        x_ref, s_ref, mask_ref, rows_ref, columns_ref, class_ref, orient_ref, class_prior_ref, orient_prior_ref,
        back_rows_ref, back_columns_ref,
    )
    copies = [pltpu.make_async_copy(a, b, sems.at[k]) for k, (a, b) in enumerate(zip(sources, targets))]
    for copy in copies:
        copy.start()
    share, crop, width = s_ref.shape
    half = width // 2
    left = lax.broadcasted_iota(jnp.int32, (crop, width), 1) < half
    for copy in copies[:3]:
        copy.wait()
    mask = mask_ref[...].astype(F32)
    mask = jnp.concatenate([mask, mask], axis=1)
    powers = []
    for j in range(share):
        s = s_ref[j].astype(F32) * mask
        turned = pltpu.roll(s, half, 1)
        first[j] = jnp.where(left, s, turned)
        second[j] = jnp.where(left, turned, -s)
        powers.append(jnp.sum(s * s, axis=0, keepdims=True))
    power = jnp.sum(jnp.concatenate(powers, axis=0), axis=1, keepdims=True)
    split_particles(x_ref, plain, swapped)
    for copy in copies[3:]:
        copy.wait()
    slot = lax.broadcasted_iota(jnp.int32, (1, share * TS), 1) // TS
    bias = jnp.zeros((1, share * TS), F32)
    start = lax.axis_index("orient") * share
    for j in range(share):
        prior = class_prior_ref[class_ref[start + j]] + orient_prior_ref[orient_ref[start + j]]
        bias = jnp.where(slot == j, prior - power[j : j + 1] * (0.5 / crop), bias)
    bias_ref[...] = jnp.broadcast_to(bias, bias_ref.shape)
    score_block(plain, swapped, first, second, bias, rows_ref, columns_ref, cross, logits_ref, lse_ref)


def score_kernel(
    x_ref, first, second, bias_ref, rows_ref, columns_ref, logits_ref, lse_ref, cross, plain, swapped
):
    split_particles(x_ref, plain, swapped)
    score_block(plain, swapped, first, second, bias_ref[:1], rows_ref, columns_ref, cross, logits_ref, lse_ref)


def log_add(a, b):
    top = jnp.maximum(a, b)
    return top + jnp.log(jnp.exp(a - top) + jnp.exp(b - top))


def to_lanes(column):
    wide = jnp.broadcast_to(column, (column.shape[0], 128))
    row = lax.broadcasted_iota(jnp.int32, wide.shape, 0)
    lane = lax.broadcasted_iota(jnp.int32, wide.shape, 1)
    return jnp.sum(jnp.where(row == lane, wide, 0.0), axis=0, keepdims=True)


def put_mass(send_ref, at, mass):
    row = lax.broadcasted_iota(jnp.int32, (8, 128), 0)
    if send_ref.dtype == F32:
        send_ref[at : at + 8] = jnp.broadcast_to(mass, (8, 128))
    else:
        high = mass.astype(BF16).astype(F32)
        middle = (mass - high).astype(BF16).astype(F32)
        low = mass - high - middle
        terms = jnp.where(row == 0, high, jnp.where(row == 1, middle, jnp.where(row == 2, low, 0.0)))
        send_ref[at : at + 16] = jnp.concatenate([terms, jnp.zeros((8, 128), F32)], axis=0).astype(BF16)


def get_mass(got_ref, at):
    if got_ref.dtype == F32:
        return got_ref[at : at + 1]
    terms = got_ref[at : at + 16].astype(F32)
    return terms[0:1] + terms[1:2] + terms[2:3]


def back_kernel(share, pack, start, last, *refs):
    refs = list(refs)
    logits_ref, lse_a_ref, lse_b_ref, x_ref, rows_ref, columns_ref = refs[:6]
    del refs[:6]
    if not start:
        re_in, im_in, mass_in = refs[:3]
        del refs[:3]
    if last:
        mask_ref, keep_ref, send_ref, mass_ref, loglik_ref = refs[:5]
        del refs[:5]
    else:
        re_ref, im_ref, mass_ref = refs[:3]
        del refs[:3]
    doubled_re, doubled_im, high, low = refs
    count, crop, width = x_ref.shape
    half = width // 2
    left = lax.broadcasted_iota(jnp.int32, (crop, width), 1) < half
    loglik = log_add(lse_a_ref[...], lse_b_ref[...])
    mass = jnp.zeros((TS, share * TS), F32)
    weights = []
    for i in range(count):
        weight = jnp.exp(logits_ref[i] - loglik[i : i + 1, :]).astype(BF16)
        mass = mass + weight.astype(F32)
        weights.append(weight)
        x = x_ref[i].astype(F32)
        turned = pltpu.roll(x, half, 1)
        doubled_re[i] = jnp.where(left, x, turned)
        doubled_im[i] = jnp.where(left, turned, x)
    mass = jnp.sum(mass, axis=0, keepdims=True)
    if not start:
        mass = mass + mass_in[:1]
    spread = jnp.dot(jnp.concatenate(weights, axis=0), rows_ref[...], preferred_element_type=F32)
    rounded = spread.astype(BF16)
    high[...] = rounded
    low[...] = (spread - rounded.astype(F32)).astype(BF16)
    forms = share * width
    wide = pack * width
    groups = share // pack
    columns = columns_ref[...]
    if last:
        mask = mask_ref[...].astype(F32)
        mask = jnp.concatenate([mask, mask], axis=1)
        sign = jnp.where(left[:1], -1.0, 1.0)
        odd = (lax.axis_index("dom") & 1) == 1
    for group in range(groups):
        re = jnp.zeros((crop, wide), F32) if start else re_in[group]
        im = jnp.zeros((crop, wide), F32) if start else im_in[group]
        for k in range(count):
            rows = slice(k * TS, (k + 1) * TS)
            here = slice(group * wide, (group + 1) * wide)
            there = slice(forms + group * wide, forms + (group + 1) * wide)
            a, b = high[rows, here], high[rows, there]
            terms = jnp.concatenate([a, b, low[rows, here], low[rows, there], a, b], axis=0)
            kernel = jnp.dot(columns, terms, preferred_element_type=F32)
            re = re + kernel * jnp.concatenate([doubled_re[k]] * pack, axis=1)
            im = im + kernel * jnp.concatenate([doubled_im[k]] * pack, axis=1)
        if not last:
            re_ref[group] = re
            im_ref[group] = im
            continue
        images = []
        for p in range(pack):
            here = slice(p * width, (p + 1) * width)
            images.append((re[:, here] + pltpu.roll(im[:, here], half, 1) * sign) * mask)
        block = 8 // pack
        tiles = [
            jnp.concatenate([image[at : at + block] for image in images], axis=0) for at in range(0, crop, block)
        ]
        for pair in range(len(tiles) // 2):
            at = (pair * groups + group) * 8
            keep_ref[at : at + 8] = jnp.where(odd, tiles[2 * pair + 1], tiles[2 * pair])
            send_ref[at : at + 8] = jnp.where(odd, tiles[2 * pair], tiles[2 * pair + 1])
    if last:
        row = lax.broadcasted_iota(jnp.int32, (share, share * TS), 0)
        lane = lax.broadcasted_iota(jnp.int32, (share, share * TS), 1)
        each = jnp.sum(jnp.where(row == lane // TS, mass, 0.0), axis=1, keepdims=True)
        mass = to_lanes(each)
        put_mass(send_ref, keep_ref.shape[0], mass)
        loglik_ref[...] = to_lanes(loglik[:, :1])[0, :count]
    mass_ref[...] = jnp.broadcast_to(mass, mass_ref.shape)


def halve_kernel(groups, bit, keep_ref, got_ref, mass_in, left_ref, send_ref, mass_ref):
    rows = keep_ref.shape[0]
    unit = groups * 8
    side = (lax.axis_index("dom") >> bit) & 1
    for pair in range(rows // unit // 2):
        at = pair * unit
        mine = pl.ds(pl.multiple_of((2 * pair + side) * unit, unit), unit)
        theirs = pl.ds(pl.multiple_of((2 * pair + 1 - side) * unit, unit), unit)
        left_ref[at : at + unit] = keep_ref[mine] + got_ref[mine].astype(F32)
        send_ref[at : at + unit] = (keep_ref[theirs] + got_ref[theirs].astype(F32)).astype(send_ref.dtype)
    mass = mass_in[:1] + get_mass(got_ref, rows)
    put_mass(send_ref, rows // 2, mass)
    mass_ref[...] = jnp.broadcast_to(mass, mass_ref.shape)


def last_kernel(groups, pack, keep_ref, got_ref, mass_in, image_ref, occupancy_ref):
    block = image_ref.shape[1]
    rows = keep_ref.shape[0]
    total = keep_ref[...] + got_ref[:rows].astype(F32)
    for g in range(groups):
        for p in range(pack):
            image_ref[p * groups + g] = total[g * 8 + p * block : g * 8 + (p + 1) * block]
    mass = mass_in[:1] + get_mass(got_ref, rows)
    occupancy_ref[...] = mass[0, : occupancy_ref.shape[0]]


def bits(count):
    return count.bit_length() - 1


def shards(n_dom, n_orient, particles, slices, freq_mask, slice_class, slice_orient, class_prior, orient_prior):
    count, crop, width = particles.shape
    share = slices.shape[0]
    lanes = share * TS
    block = crop // n_dom
    pack = 8 // block
    groups = share // pack
    vmem = pl.BlockSpec(memory_space=pltpu.VMEM)
    hbm = pl.BlockSpec(memory_space=pltpu.HBM)
    shape = jax.ShapeDtypeStruct
    params = pltpu.CompilerParams(vmem_limit_bytes=VMEM_LIMIT)
    order = [p * groups + g for g in range(groups) for p in range(pack)]
    tables = [jnp.asarray(t) for t in (*score_tables(crop, share), *back_tables(crop, share, order))]

    def call(kernel, outs, args, scratch, specs=None, flops=0, name=None):
        return pl.pallas_call(
            kernel,
            out_shape=tuple(outs),
            in_specs=specs or [vmem] * len(args),
            out_specs=(vmem,) * len(outs),
            scratch_shapes=scratch,
            compiler_params=params,
            cost_estimate=pl.CostEstimate(flops=flops, bytes_accessed=1 << 20, transcendentals=0),
            name=name,
        )(*args)

    def swap(value, axis, size, step):
        return lax.ppermute(value, axis, [(i, i ^ step) for i in range(size)])

    flops = 2 * count * crop * share * width * 2 * lanes
    scored_shapes = [shape((count, TS, lanes), F32), shape((count, 128), F32)]
    turned = pltpu.VMEM((count, crop, width), F32)
    score_scratch = [pltpu.VMEM((count * crop, share * width), BF16), turned, turned]
    slices_shape = shape(slices.shape, F32)
    score_rows, score_columns, back_rows, back_columns = tables

    slots = [particles] + [swap(particles, "orient", n_orient, r) for r in range(1, n_orient)]
    kept = (particles, freq_mask, *tables)
    logits, lse, first, second, bias, mine, mask, *tables = call(
        first_kernel,
        [*scored_shapes, slices_shape, slices_shape, shape((8, lanes), F32)]
        + [shape(value.shape, value.dtype) for value in kept],
        tuple(
            pltpu.with_memory_space_constraint(value, pltpu.HBM)
            for value in (
                particles, slices, freq_mask, score_rows, score_columns, slice_class, slice_orient, class_prior,
                orient_prior, back_rows, back_columns,
            )
        ),
        [
            pltpu.VMEM(slices.shape, slices.dtype),
            *[pltpu.SMEM(v.shape, v.dtype) for v in (slice_class, slice_orient, class_prior, orient_prior)],
            *score_scratch,
            pltpu.SemaphoreType.DMA((11,)),
        ],
        specs=[hbm] * 11, flops=flops, name="first",
    )
    score_rows, score_columns, back_rows, back_columns = tables
    slots[0] = mine
    scored = [(logits, lse)] + [
        call(
            score_kernel, scored_shapes, (parts, first, second, bias, score_rows, score_columns), score_scratch,
            flops=flops, name="score",
        )
        for parts in slots[1:]
    ]
    lses = [s[1] for s in scored]
    for b in range(bits(n_orient)):
        theirs = [swap(lses[r ^ (1 << b)], "orient", n_orient, 1 << b) for r in range(n_orient)]
        if b < bits(n_orient) - 1:
            lses = [log_add(x, y) for x, y in zip(lses, theirs)]

    rows = crop // block * groups * 8
    steps = bits(n_dom)

    def sent(step, height):
        dtype = F32 if step in (0, steps - 1) else BF16
        return shape((height + (8 if dtype == F32 else 16), width), dtype)

    sums = shape((groups, crop, pack * width), F32)
    mass_shape = shape((8, lanes), F32)
    back_scratch = [turned, turned] + [pltpu.VMEM((count * TS, 2 * share * width), BF16)] * 2
    partial = ()
    for r in range(1, n_orient):
        partial = call(
            functools.partial(back_kernel, share, pack, r == 1, False),
            [sums, sums, mass_shape],
            (scored[r][0], lses[r], theirs[r], slots[r], back_rows, back_columns, *partial),
            back_scratch, flops=flops, name="back",
        )
    keep, send, mass, loglik = call(
        functools.partial(back_kernel, share, pack, False, True),
        [shape((rows // 2, width), F32), sent(0, rows // 2), shape((8, 128), F32), shape((count,), F32)],
        (scored[0][0], lses[0], theirs[0], slots[0], back_rows, back_columns, *partial, mask),
        back_scratch, flops=flops, name="last_back",
    )
    for b in range(steps - 1):
        got = swap(send, "dom", n_dom, 1 << b)
        height = keep.shape[0] // 2
        keep, send, mass = call(
            functools.partial(halve_kernel, groups, b + 1),
            [shape((height, width), F32), sent(b + 1, height), shape((8, 128), F32)],
            (keep, got, mass), [], name="halve",
        )
    got = swap(send, "dom", n_dom, n_dom // 2)
    image, occupancy = call(
        functools.partial(last_kernel, groups, pack),
        [shape((share, block, width), F32), shape((share,), F32)],
        (keep, got, mass), [], name="last",
    )
    return image, occupancy, loglik


def solution(mesh):
    placed = (P(("dom", "orient"), None, None), P("orient", None, None), P(), P(), P(), P(), P())
    return jax.shard_map(
        functools.partial(shards, mesh.shape["dom"], mesh.shape["orient"]),
        mesh=mesh,
        in_specs=placed,
        out_specs=(P("orient", "dom", None), P("orient"), P(("dom", "orient"))),
        check_vma=False,
    )
```

```python
import functools
import math

import jax
import jax.numpy as jnp
import ml_dtypes
import numpy as np
from jax import lax
from jax.experimental import pallas as pl
from jax.experimental.pallas import tpu as pltpu
from jax.sharding import PartitionSpec as P

TS = 16
F32 = jnp.float32
BF16 = jnp.bfloat16
VMEM_LIMIT = 24 * 1024 * 1024


def phase_tables(crop):
    freq = np.arange(crop, dtype=np.float64) - crop // 2
    offset = np.arange(TS, dtype=np.float64) - TS // 2
    angle = 2.0 * math.pi / crop * freq[:, None] * offset[None, :]
    return np.cos(angle).astype(np.float32), np.sin(angle).astype(np.float32)


def high_low(table):
    high = table.astype(ml_dtypes.bfloat16)
    low = (table - high.astype(np.float32)).astype(ml_dtypes.bfloat16)
    return high, low


def score_tables(crop, share):
    cosine, sine = phase_tables(crop)
    rows = np.zeros((share, 2, crop, 2, share, TS), np.float32)
    for j in range(share):
        rows[j, 0, :, 0, j] = cosine
        rows[j, 0, :, 1, j] = sine
        rows[j, 1, :, 0, j] = -sine
        rows[j, 1, :, 1, j] = cosine
    rows = rows.reshape(share * 2 * crop, 2 * share * TS).astype(ml_dtypes.bfloat16)
    high, low = high_low(np.concatenate([cosine.T, -sine.T], axis=1))
    columns = np.concatenate(
        [np.concatenate([high, high], axis=1), np.concatenate([low, np.zeros_like(low)], axis=1)], axis=0
    )
    return rows, columns


def back_tables(crop, share, order):
    cosine, sine = phase_tables(crop)
    rows = np.zeros((share, TS, 2, share, 2, crop), np.float32)
    for place, j in enumerate(order):
        rows[j, :, 0, place, 0] = cosine.T
        rows[j, :, 0, place, 1] = -sine.T
        rows[j, :, 1, place, 0] = -sine.T
        rows[j, :, 1, place, 1] = -cosine.T
    rows = rows.reshape(share * TS, 2 * share * 2 * crop).astype(ml_dtypes.bfloat16)
    high, low = high_low(np.concatenate([cosine, sine], axis=1))
    return rows, np.concatenate([high, high, low], axis=1)


def score_block(x_ref, first_ref, second_ref, bias, rows_ref, columns_ref, logits_ref, lse_ref):
    count, crop, width = x_ref.shape
    share = first_ref.shape[0]
    lanes = share * TS
    cross = []
    for i in range(count):
        x = x_ref[i].astype(F32)
        turned = pltpu.roll(x, width // 2, 1)
        terms = [(x * first_ref[j] + turned * second_ref[j]).astype(BF16) for j in range(share)]
        cross.append(jnp.concatenate(terms, axis=1))
    rowcorr = jnp.dot(jnp.concatenate(cross, axis=0), rows_ref[...], preferred_element_type=F32)
    high = rowcorr.astype(BF16)
    low = (rowcorr - high.astype(F32)).astype(BF16)
    stacked = jnp.concatenate(
        [
            jnp.concatenate(
                [part[i * crop : (i + 1) * crop, k * lanes : (k + 1) * lanes] for part in (high, low) for k in (0, 1)],
                axis=0,
            )
            for i in range(count)
        ],
        axis=1,
    )
    corr = jnp.dot(columns_ref[...], stacked, preferred_element_type=F32)
    corr = (corr[:TS] + corr[TS:]) * (1.0 / crop)
    logits = [corr[:, i * lanes : (i + 1) * lanes] + bias for i in range(count)]
    for i in range(count):
        logits_ref[i] = logits[i]
    tops = jnp.concatenate([jnp.max(value, axis=0, keepdims=True) for value in logits], axis=0)
    top = jnp.max(tops, axis=1, keepdims=True)
    sums = [jnp.sum(jnp.exp(logits[i] - top[i : i + 1]), axis=0, keepdims=True) for i in range(count)]
    total = jnp.sum(jnp.concatenate(sums, axis=0), axis=1, keepdims=True)
    lse_ref[...] = jnp.broadcast_to(top + jnp.log(total), lse_ref.shape)


def prepare_slices(s_ref, mask_ref, first, second):
    share, crop, width = s_ref.shape
    half = width // 2
    left = lax.broadcasted_iota(jnp.int32, (crop, width), 1) < half
    mask = mask_ref[...].astype(F32)
    mask = jnp.concatenate([mask, mask], axis=1)
    powers = []
    for j in range(share):
        s = s_ref[j].astype(F32) * mask
        turned = pltpu.roll(s, half, 1)
        first[j] = jnp.where(left, s, turned)
        second[j] = jnp.where(left, turned, -s)
        powers.append(jnp.sum(s * s, axis=0, keepdims=True))
    power = jnp.sum(jnp.concatenate(powers, axis=0), axis=1, keepdims=True) * (0.5 / crop)
    slot = lax.broadcasted_iota(jnp.int32, (1, share * TS), 1) // TS
    spread = jnp.zeros((1, share * TS), F32)
    for j in range(share):
        spread = jnp.where(slot == j, power[j : j + 1], spread)
    return spread


def first_kernel(*refs):
    sources, (logits_ref, lse_ref, first, second, bias_ref), kept = refs[:11], refs[11:16], refs[16:22]
    s_ref, class_ref, orient_ref, class_prior_ref, orient_prior_ref, sems = refs[22:]
    x_ref, mask_ref, rows_ref, columns_ref, back_rows_ref, back_columns_ref = kept
    targets = (
        class_ref, orient_ref, class_prior_ref, orient_prior_ref, x_ref, s_ref, mask_ref, rows_ref, columns_ref,
        back_rows_ref, back_columns_ref,
    )
    copies = [pltpu.make_async_copy(a, b, sems.at[k]) for k, (a, b) in enumerate(zip(sources, targets))]
    for copy in copies:
        copy.start()
    share = s_ref.shape[0]
    for copy in copies[:4]:
        copy.wait()
    slot = lax.broadcasted_iota(jnp.int32, (1, share * TS), 1) // TS
    prior = jnp.zeros((1, share * TS), F32)
    start = lax.axis_index("orient") * share
    for j in range(share):
        value = class_prior_ref[class_ref[start + j]] + orient_prior_ref[orient_ref[start + j]]
        prior = jnp.where(slot == j, value, prior)
    for copy in copies[4:7]:
        copy.wait()
    power = prepare_slices(s_ref, mask_ref, first, second)
    for copy in copies[7:9]:
        copy.wait()
    bias = prior - power
    bias_ref[...] = jnp.broadcast_to(bias, bias_ref.shape)
    score_block(x_ref, first, second, bias, rows_ref, columns_ref, logits_ref, lse_ref)
    for copy in copies[9:]:
        copy.wait()


def score_kernel(x_ref, first, second, bias_ref, rows_ref, columns_ref, logits_ref, lse_ref):
    score_block(x_ref, first, second, bias_ref[:1], rows_ref, columns_ref, logits_ref, lse_ref)


def log_add(a, b):
    top = jnp.maximum(a, b)
    return top + jnp.log(jnp.exp(a - top) + jnp.exp(b - top))


def parity(index, limit):
    total = index & 1
    for b in range(1, bits(limit)):
        total = total ^ ((index >> b) & 1)
    return total


def to_lanes(column):
    wide = jnp.broadcast_to(column, (column.shape[0], 128))
    row = lax.broadcasted_iota(jnp.int32, wide.shape, 0)
    lane = lax.broadcasted_iota(jnp.int32, wide.shape, 1)
    return jnp.sum(jnp.where(row == lane, wide, 0.0), axis=0, keepdims=True)


def put_mass(send_ref, at, mass):
    row = lax.broadcasted_iota(jnp.int32, (8, 128), 0)
    if send_ref.dtype == F32:
        send_ref[at : at + 8] = jnp.broadcast_to(mass, (8, 128))
    else:
        high = mass.astype(BF16).astype(F32)
        middle = (mass - high).astype(BF16).astype(F32)
        low = mass - high - middle
        terms = jnp.where(row == 0, high, jnp.where(row == 1, middle, jnp.where(row == 2, low, 0.0)))
        send_ref[at : at + 16] = jnp.concatenate([terms, jnp.zeros((8, 128), F32)], axis=0).astype(BF16)


def get_mass(got_ref, at):
    if got_ref.dtype == F32:
        return got_ref[at : at + 1]
    terms = got_ref[at : at + 16].astype(F32)
    return terms[0:1] + terms[1:2] + terms[2:3]


def back_kernel(share, pack, n_lse, start, last, *refs):
    refs = list(refs)
    logits_ref, x_ref, rows_ref, columns_ref = refs[:4]
    lse_refs = refs[4 : 4 + n_lse]
    del refs[: 4 + n_lse]
    if not start:
        re_in, im_in, mass_in = refs[:3]
        del refs[:3]
    if last:
        mask_ref, keep_ref, send_ref, mass_ref, loglik_ref = refs[:5]
        del refs[:5]
    else:
        re_ref, im_ref, mass_ref = refs[:3]
        del refs[:3]
    doubled_re, doubled_im, high, low = refs
    count, crop, width = x_ref.shape
    half = width // 2
    left = lax.broadcasted_iota(jnp.int32, (crop, width), 1) < half
    loglik = functools.reduce(log_add, [ref[...] for ref in lse_refs])
    mass = jnp.zeros((TS, share * TS), F32)
    weights = []
    for i in range(count):
        weight = jnp.exp(logits_ref[i] - loglik[i : i + 1, :]).astype(BF16)
        mass = mass + weight.astype(F32)
        weights.append(weight)
        x = x_ref[i].astype(F32)
        turned = pltpu.roll(x, half, 1)
        doubled_re[i] = jnp.where(left, x, turned)
        doubled_im[i] = jnp.where(left, turned, x)
    mass = jnp.sum(mass, axis=0, keepdims=True)
    if not start:
        mass = mass + mass_in[:1]
    spread = jnp.dot(jnp.concatenate(weights, axis=0), rows_ref[...], preferred_element_type=F32)
    rounded = spread.astype(BF16)
    high[...] = rounded
    low[...] = (spread - rounded.astype(F32)).astype(BF16)
    forms = share * width
    wide = pack * width
    groups = share // pack
    columns = columns_ref[...]
    if last:
        mask = mask_ref[...].astype(F32)
        mask = jnp.concatenate([mask, mask], axis=1)
        sign = jnp.where(left[:1], -1.0, 1.0)
        odd = parity(lax.axis_index("dom"), crop * pack // 8)
    for group in range(groups):
        re = jnp.zeros((crop, wide), F32) if start else re_in[group]
        im = jnp.zeros((crop, wide), F32) if start else im_in[group]
        for k in range(count):
            rows = slice(k * TS, (k + 1) * TS)
            here = slice(group * wide, (group + 1) * wide)
            there = slice(forms + group * wide, forms + (group + 1) * wide)
            a, b = high[rows, here], high[rows, there]
            terms = jnp.concatenate([a, b, low[rows, here], low[rows, there], a, b], axis=0)
            kernel = jnp.dot(columns, terms, preferred_element_type=F32)
            re = re + kernel * jnp.concatenate([doubled_re[k]] * pack, axis=1)
            im = im + kernel * jnp.concatenate([doubled_im[k]] * pack, axis=1)
        if not last:
            re_ref[group] = re
            im_ref[group] = im
            continue
        images = []
        for p in range(pack):
            here = slice(p * width, (p + 1) * width)
            images.append((re[:, here] + pltpu.roll(im[:, here], half, 1) * sign) * mask)
        block = 8 // pack
        tiles = [
            jnp.concatenate([image[at : at + block] for image in images], axis=0) for at in range(0, crop, block)
        ]
        for pair in range(len(tiles) // 2):
            at = (pair * groups + group) * 8
            even, other = tiles[2 * pair], tiles[2 * pair + 1]
            if parity(pair, crop):
                even, other = other, even
            keep_ref[at : at + 8] = jnp.where(odd == 1, other, even)
            send_ref[at : at + 8] = jnp.where(odd == 1, even, other)
    if last:
        row = lax.broadcasted_iota(jnp.int32, (share, share * TS), 0)
        lane = lax.broadcasted_iota(jnp.int32, (share, share * TS), 1)
        each = jnp.sum(jnp.where(row == lane // TS, mass, 0.0), axis=1, keepdims=True)
        mass = to_lanes(each)
        put_mass(send_ref, keep_ref.shape[0], mass)
        loglik_ref[...] = jnp.broadcast_to(to_lanes(loglik[:, :1]), loglik_ref.shape)
    mass_ref[...] = jnp.broadcast_to(mass, mass_ref.shape)


def halve_kernel(groups, bit, keep_ref, got_ref, mass_in, left_ref, send_ref, mass_ref):
    rows = keep_ref.shape[0]
    unit = groups * 8
    side = (lax.axis_index("dom") >> bit) & 1
    for pair in range(rows // unit // 2):
        at = pair * unit
        mine = pl.ds(pl.multiple_of((2 * pair + side) * unit, unit), unit)
        theirs = pl.ds(pl.multiple_of((2 * pair + 1 - side) * unit, unit), unit)
        left_ref[at : at + unit] = keep_ref[mine] + got_ref[mine].astype(F32)
        send_ref[at : at + unit] = (keep_ref[theirs] + got_ref[theirs].astype(F32)).astype(send_ref.dtype)
    mass = mass_in[:1] + get_mass(got_ref, rows)
    put_mass(send_ref, rows // 2, mass)
    mass_ref[...] = jnp.broadcast_to(mass, mass_ref.shape)


def last_kernel(groups, pack, keep_ref, got_ref, mass_in, loglik_in, image_ref, occupancy_ref, loglik_ref):
    block = image_ref.shape[1]
    rows = keep_ref.shape[0]
    total = keep_ref[...] + got_ref[:rows].astype(F32)
    for g in range(groups):
        for p in range(pack):
            image_ref[p * groups + g] = total[g * 8 + p * block : g * 8 + (p + 1) * block]
    mass = mass_in[:1] + get_mass(got_ref, rows)
    occupancy_ref[...] = mass[0, : occupancy_ref.shape[0]]
    loglik_ref[...] = loglik_in[0, : loglik_ref.shape[0]]


def bits(count):
    return count.bit_length() - 1


def shards(n_dom, n_orient, particles, slices, freq_mask, slice_class, slice_orient, class_prior, orient_prior):
    count, crop, width = particles.shape
    share = slices.shape[0]
    lanes = share * TS
    block = crop // n_dom
    pack = 8 // block
    groups = share // pack
    vmem = pl.BlockSpec(memory_space=pltpu.VMEM)
    hbm = pl.BlockSpec(memory_space=pltpu.HBM)
    shape = jax.ShapeDtypeStruct
    params = pltpu.CompilerParams(vmem_limit_bytes=VMEM_LIMIT)
    order = [p * groups + g for g in range(groups) for p in range(pack)]
    tables = [jnp.asarray(t) for t in (*score_tables(crop, share), *back_tables(crop, share, order))]

    def call(kernel, outs, args, scratch, specs=None, flops=0, name=None):
        return pl.pallas_call(
            kernel,
            out_shape=tuple(outs),
            in_specs=specs or [vmem] * len(args),
            out_specs=(vmem,) * len(outs),
            scratch_shapes=scratch,
            compiler_params=params,
            cost_estimate=pl.CostEstimate(flops=flops, bytes_accessed=1 << 20, transcendentals=0),
            name=name,
        )(*args)

    def swap(value, r):
        core = parity(r, n_orient)
        pairs = [(d * n_orient + o, (d ^ core) * n_orient + (o ^ r)) for d in range(n_dom) for o in range(n_orient)]
        return lax.ppermute(value, ("dom", "orient"), pairs)

    flops = 2 * count * crop * share * width * 2 * lanes
    logits_shape, lse_shape = shape((count, TS, lanes), F32), shape((count, 128), F32)
    slices_shape = shape(slices.shape, F32)
    score_rows, score_columns, back_rows, back_columns = tables

    slots = [particles] + [swap(particles, r) for r in range(1, n_orient)]
    kept = (particles, freq_mask, *tables)
    logits, lse, first, second, bias, mine, mask, *tables = call(
        first_kernel,
        [logits_shape, lse_shape, slices_shape, slices_shape, shape((8, lanes), F32)]
        + [shape(value.shape, value.dtype) for value in kept],
        tuple(
            pltpu.with_memory_space_constraint(value, pltpu.HBM)
            for value in (
                slice_class, slice_orient, class_prior, orient_prior, particles, slices, freq_mask, score_rows,
                score_columns, back_rows, back_columns,
            )
        ),
        [
            pltpu.VMEM(slices.shape, slices.dtype),
            *[pltpu.SMEM(v.shape, v.dtype) for v in (slice_class, slice_orient, class_prior, orient_prior)],
            pltpu.SemaphoreType.DMA((11,)),
        ],
        specs=[hbm] * 11, flops=flops, name="first",
    )
    score_rows, score_columns, back_rows, back_columns = tables
    slots[0] = mine
    scored = [(logits, lse)] + [
        call(
            score_kernel, [logits_shape, lse_shape], (parts, first, second, bias, score_rows, score_columns), [],
            flops=flops, name="score",
        )
        for parts in slots[1:]
    ]
    terms = [[s[1]] for s in scored]
    for b in range(bits(n_orient)):
        sums = [functools.reduce(log_add, t) for t in terms]
        terms = [[sums[r], swap(sums[r ^ (1 << b)], 1 << b)] for r in range(n_orient)]

    rows = crop // block * groups * 8
    steps = bits(n_dom)

    def sent(step, height):
        dtype = F32 if step in (0, steps - 1) else BF16
        return shape((height + (8 if dtype == F32 else 16), width), dtype)

    sums = shape((groups, crop, pack * width), F32)
    mass_shape = shape((8, lanes), F32)
    turned = pltpu.VMEM((count, crop, width), F32)
    back_scratch = [turned, turned] + [pltpu.VMEM((count * TS, 2 * share * width), BF16)] * 2
    partial = ()
    for r in range(1, n_orient):
        partial = call(
            functools.partial(back_kernel, share, pack, len(terms[r]), r == 1, False),
            [sums, sums, mass_shape],
            (scored[r][0], slots[r], back_rows, back_columns, *terms[r], *partial),
            back_scratch, flops=flops, name="back",
        )
    keep, send, mass, loglik = call(
        functools.partial(back_kernel, share, pack, len(terms[0]), False, True),
        [shape((rows // 2, width), F32), sent(0, rows // 2), shape((8, 128), F32), shape((8, 128), F32)],
        (scored[0][0], slots[0], back_rows, back_columns, *terms[0], *partial, mask),
        back_scratch, flops=flops, name="last_back",
    )
    def exchange(value, b):
        step = 1 << b | 1
        return lax.ppermute(value, "dom", [(i, i ^ step) for i in range(n_dom)])

    for b in range(steps - 1):
        got = exchange(send, b)
        height = keep.shape[0] // 2
        keep, send, mass = call(
            functools.partial(halve_kernel, groups, b + 1),
            [shape((height, width), F32), sent(b + 1, height), shape((8, 128), F32)],
            (keep, got, mass), [], name="halve",
        )
    got = exchange(send, steps - 1)
    image, occupancy, loglik = call(
        functools.partial(last_kernel, groups, pack),
        [shape((share, block, width), F32), shape((share,), F32), shape((count,), F32)],
        (keep, got, mass, loglik), [], name="last",
    )
    return image, occupancy, loglik


def solution(mesh):
    placed = (P(("dom", "orient"), None, None), P("orient", None, None), P(), P(), P(), P(), P())
    return jax.shard_map(
        functools.partial(shards, mesh.shape["dom"], mesh.shape["orient"]),
        mesh=mesh,
        in_specs=placed,
        out_specs=(P("orient", "dom", None), P("orient"), P(("dom", "orient"))),
        check_vma=False,
    )
```

```python
import functools
import math

import jax
import jax.numpy as jnp
import ml_dtypes
import numpy as np
from jax import lax
from jax.experimental import pallas as pl
from jax.experimental.pallas import tpu as pltpu
from jax.sharding import PartitionSpec as P

TS = 16
F32 = jnp.float32
BF16 = jnp.bfloat16
VMEM_LIMIT = 24 * 1024 * 1024


def phase_tables(crop):
    freq = np.arange(crop, dtype=np.float64) - crop // 2
    offset = np.arange(TS, dtype=np.float64) - TS // 2
    angle = 2.0 * math.pi / crop * freq[:, None] * offset[None, :]
    return np.cos(angle).astype(np.float32), np.sin(angle).astype(np.float32)


def high_low(table):
    high = table.astype(ml_dtypes.bfloat16)
    low = (table - high.astype(np.float32)).astype(ml_dtypes.bfloat16)
    return high, low


def score_tables(crop, share):
    cosine, sine = phase_tables(crop)
    rows = np.zeros((share, 2, crop, 2, share, TS), np.float32)
    for j in range(share):
        rows[j, 0, :, 0, j] = cosine
        rows[j, 0, :, 1, j] = sine
        rows[j, 1, :, 0, j] = -sine
        rows[j, 1, :, 1, j] = cosine
    rows = rows.reshape(share * 2 * crop, 2 * share * TS).astype(ml_dtypes.bfloat16)
    high, low = high_low(np.concatenate([cosine.T, -sine.T], axis=1))
    columns = np.concatenate(
        [np.concatenate([high, high], axis=1), np.concatenate([low, np.zeros_like(low)], axis=1)], axis=0
    )
    return rows, columns


def back_tables(crop, share, order):
    cosine, sine = phase_tables(crop)
    rows = np.zeros((share, TS, 2, share, 2, crop), np.float32)
    for place, j in enumerate(order):
        rows[j, :, 0, place, 0] = cosine.T
        rows[j, :, 0, place, 1] = -sine.T
        rows[j, :, 1, place, 0] = -sine.T
        rows[j, :, 1, place, 1] = -cosine.T
    rows = rows.reshape(share * TS, 2 * share * 2 * crop).astype(ml_dtypes.bfloat16)
    high, low = high_low(np.concatenate([cosine, sine], axis=1))
    return rows, np.concatenate([high, high, low], axis=1)


def score_block(x_ref, first_ref, second_ref, bias, rows_ref, columns_ref, logits_ref, lse_ref):
    count, crop, width = x_ref.shape
    share = first_ref.shape[0]
    lanes = share * TS
    cross = []
    for i in range(count):
        x = x_ref[i].astype(F32)
        turned = pltpu.roll(x, width // 2, 1)
        terms = [(x * first_ref[j] + turned * second_ref[j]).astype(BF16) for j in range(share)]
        cross.append(jnp.concatenate(terms, axis=1))
    rowcorr = jnp.dot(jnp.concatenate(cross, axis=0), rows_ref[...], preferred_element_type=F32)
    high = rowcorr.astype(BF16)
    low = (rowcorr - high.astype(F32)).astype(BF16)
    stacked = jnp.concatenate(
        [
            jnp.concatenate(
                [part[i * crop : (i + 1) * crop, k * lanes : (k + 1) * lanes] for part in (high, low) for k in (0, 1)],
                axis=0,
            )
            for i in range(count)
        ],
        axis=1,
    )
    corr = jnp.dot(columns_ref[...], stacked, preferred_element_type=F32)
    corr = (corr[:TS] + corr[TS:]) * (1.0 / crop)
    logits = [corr[:, i * lanes : (i + 1) * lanes] + bias for i in range(count)]
    for i in range(count):
        logits_ref[i] = logits[i]
    tops = jnp.concatenate([jnp.max(value, axis=0, keepdims=True) for value in logits], axis=0)
    top = jnp.max(tops, axis=1, keepdims=True)
    sums = [jnp.sum(jnp.exp(logits[i] - top[i : i + 1]), axis=0, keepdims=True) for i in range(count)]
    total = jnp.sum(jnp.concatenate(sums, axis=0), axis=1, keepdims=True)
    lse_ref[...] = jnp.broadcast_to(top + jnp.log(total), lse_ref.shape)


def prepare_slices(s_ref, mask_ref, first, second):
    share, crop, width = s_ref.shape
    half = width // 2
    left = lax.broadcasted_iota(jnp.int32, (crop, width), 1) < half
    mask = mask_ref[...].astype(F32)
    mask = jnp.concatenate([mask, mask], axis=1)
    powers = []
    for j in range(share):
        s = s_ref[j].astype(F32) * mask
        turned = pltpu.roll(s, half, 1)
        first[j] = jnp.where(left, s, turned)
        second[j] = jnp.where(left, turned, -s)
        powers.append(jnp.sum(s * s, axis=0, keepdims=True))
    power = jnp.sum(jnp.concatenate(powers, axis=0), axis=1, keepdims=True) * (0.5 / crop)
    slot = lax.broadcasted_iota(jnp.int32, (1, share * TS), 1) // TS
    spread = jnp.zeros((1, share * TS), F32)
    for j in range(share):
        spread = jnp.where(slot == j, power[j : j + 1], spread)
    return spread


def first_kernel(*refs):
    sources, (logits_ref, lse_ref, first, second, bias_ref), kept = refs[:11], refs[11:16], refs[16:22]
    s_ref, class_ref, orient_ref, class_prior_ref, orient_prior_ref, sems = refs[22:]
    x_ref, mask_ref, rows_ref, columns_ref, back_rows_ref, back_columns_ref = kept
    targets = (
        class_ref, orient_ref, class_prior_ref, orient_prior_ref, x_ref, s_ref, mask_ref, rows_ref, columns_ref,
        back_rows_ref, back_columns_ref,
    )
    copies = [pltpu.make_async_copy(a, b, sems.at[k]) for k, (a, b) in enumerate(zip(sources, targets))]
    for copy in copies:
        copy.start()
    share = s_ref.shape[0]
    for copy in copies[:4]:
        copy.wait()
    slot = lax.broadcasted_iota(jnp.int32, (1, share * TS), 1) // TS
    prior = jnp.zeros((1, share * TS), F32)
    start = lax.axis_index("orient") * share
    for j in range(share):
        value = class_prior_ref[class_ref[start + j]] + orient_prior_ref[orient_ref[start + j]]
        prior = jnp.where(slot == j, value, prior)
    for copy in copies[4:7]:
        copy.wait()
    power = prepare_slices(s_ref, mask_ref, first, second)
    for copy in copies[7:9]:
        copy.wait()
    bias = prior - power
    bias_ref[...] = jnp.broadcast_to(bias, bias_ref.shape)
    score_block(x_ref, first, second, bias, rows_ref, columns_ref, logits_ref, lse_ref)
    for copy in copies[9:]:
        copy.wait()


def score_kernel(x_ref, first, second, bias_ref, rows_ref, columns_ref, logits_ref, lse_ref):
    score_block(x_ref, first, second, bias_ref[:1], rows_ref, columns_ref, logits_ref, lse_ref)


def log_add(a, b):
    top = jnp.maximum(a, b)
    return top + jnp.log(jnp.exp(a - top) + jnp.exp(b - top))


def parity(index, limit):
    total = index & 1
    for b in range(1, bits(limit)):
        total = total ^ ((index >> b) & 1)
    return total


def to_lanes(column):
    wide = jnp.broadcast_to(column, (column.shape[0], 128))
    row = lax.broadcasted_iota(jnp.int32, wide.shape, 0)
    lane = lax.broadcasted_iota(jnp.int32, wide.shape, 1)
    return jnp.sum(jnp.where(row == lane, wide, 0.0), axis=0, keepdims=True)


def put_mass(send_ref, at, mass):
    row = lax.broadcasted_iota(jnp.int32, (8, 128), 0)
    if send_ref.dtype == F32:
        send_ref[at : at + 8] = jnp.broadcast_to(mass, (8, 128))
    else:
        high = mass.astype(BF16).astype(F32)
        middle = (mass - high).astype(BF16).astype(F32)
        low = mass - high - middle
        terms = jnp.where(row == 0, high, jnp.where(row == 1, middle, jnp.where(row == 2, low, 0.0)))
        send_ref[at : at + 16] = jnp.concatenate([terms, jnp.zeros((8, 128), F32)], axis=0).astype(BF16)


def get_mass(got_ref, at):
    if got_ref.dtype == F32:
        return got_ref[at : at + 1]
    terms = got_ref[at : at + 16].astype(F32)
    return terms[0:1] + terms[1:2] + terms[2:3]


def double_particles(x_ref, doubled_re, doubled_im):
    count, crop, width = x_ref.shape
    left = lax.broadcasted_iota(jnp.int32, (crop, width), 1) < width // 2
    for i in range(count):
        x = x_ref[i].astype(F32)
        turned = pltpu.roll(x, width // 2, 1)
        doubled_re[i] = jnp.where(left, x, turned)
        doubled_im[i] = jnp.where(left, turned, x)


def put_spread(spread, high, low):
    rounded = spread.astype(BF16)
    high[...] = rounded
    low[...] = (spread - rounded.astype(F32)).astype(BF16)


def kernel_of(high, low, columns, k, group, wide):
    rows = slice(k * TS, (k + 1) * TS)
    here = slice(group * wide, (group + 1) * wide)
    there = slice(high.shape[1] // 2 + group * wide, high.shape[1] // 2 + (group + 1) * wide)
    a, b = high[rows, here], high[rows, there]
    terms = jnp.concatenate([a, b, low[rows, here], low[rows, there], a, b], axis=0)
    return jnp.dot(columns, terms, preferred_element_type=F32)


def put_images(re, im, mask, odd, pack, group, groups, out_ref, at):
    crop, width = mask.shape
    half = width // 2
    signed = jnp.where(lax.broadcasted_iota(jnp.int32, (1, width), 1) < half, -mask, mask)
    images = []
    for p in range(pack):
        here = slice(p * width, (p + 1) * width)
        images.append(re[:, here] * mask + pltpu.roll(im[:, here], half, 1) * signed)
    block = 8 // pack
    tiles = [jnp.concatenate([image[r : r + block] for image in images], axis=0) for r in range(0, crop, block)]
    pairs = len(tiles) // 2
    for pair in range(pairs):
        even, other = tiles[2 * pair], tiles[2 * pair + 1]
        if parity(pair, crop):
            even, other = other, even
        kept, given = at + (pair * groups + group) * 8, at + ((pairs + pair) * groups + group) * 8
        out_ref[kept : kept + 8] = jnp.where(odd == 1, other, even)
        out_ref[given : given + 8] = jnp.where(odd == 1, even, other)


def twice_mask(mask_ref):
    mask = mask_ref[...].astype(F32)
    return jnp.concatenate([mask, mask], axis=1)


def own_kernel(
    share, pack, logits_ref, lse_ref, x_ref, mask_ref, rows_ref, columns_ref, out_ref, doubled_re, doubled_im, high, low
):
    count, crop, width = x_ref.shape
    double_particles(x_ref, doubled_re, doubled_im)
    weights = jnp.concatenate([jnp.exp(logits_ref[i] - lse_ref[i : i + 1, :]) for i in range(count)], axis=0)
    rounded = weights.astype(BF16)
    rest = (weights - rounded.astype(F32)).astype(BF16)
    rows = rows_ref[...]
    put_spread(
        jnp.dot(rounded, rows, preferred_element_type=F32) + jnp.dot(rest, rows, preferred_element_type=F32), high, low
    )
    columns = columns_ref[...]
    mask = twice_mask(mask_ref)
    odd = parity(lax.axis_index("dom"), crop * pack // 8)
    height = crop * share
    for group in range(share // pack):
        for k in range(count):
            kernel = kernel_of(high, low, columns, k, group, pack * width)
            re = kernel * jnp.concatenate([doubled_re[k]] * pack, axis=1)
            im = kernel * jnp.concatenate([doubled_im[k]] * pack, axis=1)
            put_images(re, im, mask, odd, pack, group, share // pack, out_ref, k * height)


def back_kernel(share, pack, start, n_lse, *refs):
    refs = list(refs)
    logits_ref, x_ref, mask_ref, rows_ref, columns_ref = refs[:5]
    lse_refs = refs[5 : 5 + n_lse]
    del refs[: 5 + n_lse]
    if not start:
        out_in, mass_in = refs[:2]
        del refs[:2]
    out_ref, mass_ref, doubled_re, doubled_im, high, low = refs
    count, crop, width = x_ref.shape
    loglik = functools.reduce(log_add, [ref[...] for ref in lse_refs])
    double_particles(x_ref, doubled_re, doubled_im)
    mass = jnp.zeros((TS, share * TS), F32)
    weights = []
    for i in range(count):
        weight = jnp.exp(logits_ref[i] - loglik[i : i + 1, :]).astype(BF16)
        mass = mass + weight.astype(F32)
        weights.append(weight)
    mass = jnp.sum(mass, axis=0, keepdims=True)
    if not start:
        mass = mass + mass_in[:1]
    mass_ref[...] = jnp.broadcast_to(mass, mass_ref.shape)
    put_spread(jnp.dot(jnp.concatenate(weights, axis=0), rows_ref[...], preferred_element_type=F32), high, low)
    wide = pack * width
    columns = columns_ref[...]
    mask = twice_mask(mask_ref)
    odd = parity(lax.axis_index("dom"), crop * pack // 8)
    for group in range(share // pack):
        re = jnp.zeros((crop, wide), F32)
        im = jnp.zeros((crop, wide), F32)
        for k in range(count):
            kernel = kernel_of(high, low, columns, k, group, wide)
            re = re + kernel * jnp.concatenate([doubled_re[k]] * pack, axis=1)
            im = im + kernel * jnp.concatenate([doubled_im[k]] * pack, axis=1)
        put_images(re, im, mask, odd, pack, group, share // pack, out_ref, 0)
    if not start:
        out_ref[...] = out_ref[...] + out_in[...]


def last_back_kernel(share, n_lse, logits_ref, lse_ref, own_ref, sum_ref, mass_in, *refs):
    lse_refs = refs[:n_lse]
    keep_ref, send_ref, mass_ref, loglik_ref = refs[n_lse:]
    count = logits_ref.shape[0]
    loglik = functools.reduce(log_add, [ref[...] for ref in lse_refs])
    factor = jnp.exp(lse_ref[...] - loglik)
    mass = jnp.zeros((TS, share * TS), F32)
    for i in range(count):
        mass = mass + jnp.exp(logits_ref[i] - loglik[i : i + 1, :]).astype(BF16).astype(F32)
    mass = jnp.sum(mass, axis=0, keepdims=True) + mass_in[:1]
    row = lax.broadcasted_iota(jnp.int32, (share, share * TS), 0)
    lane = lax.broadcasted_iota(jnp.int32, (share, share * TS), 1)
    mass = to_lanes(jnp.sum(jnp.where(row == lane // TS, mass, 0.0), axis=1, keepdims=True))
    height = sum_ref.shape[0]
    half = height // 2
    factors = [jnp.broadcast_to(factor[i : i + 1, :], (8, factor.shape[1])) for i in range(count)]
    for at in range(0, height, 8):
        total = sum_ref[at : at + 8]
        for i in range(count):
            total = total + own_ref[i * height + at : i * height + at + 8] * factors[i]
        if at < half:
            keep_ref[at : at + 8] = total
        else:
            send_ref[at - half : at - half + 8] = total
    put_mass(send_ref, half, mass)
    loglik_ref[...] = jnp.broadcast_to(to_lanes(loglik[:, :1]), loglik_ref.shape)
    mass_ref[...] = jnp.broadcast_to(mass, mass_ref.shape)


def halve_kernel(groups, bit, keep_ref, got_ref, mass_in, left_ref, send_ref, mass_ref):
    rows = keep_ref.shape[0]
    unit = groups * 8
    side = (lax.axis_index("dom") >> bit) & 1
    for pair in range(rows // unit // 2):
        at = pair * unit
        mine = pl.ds(pl.multiple_of((2 * pair + side) * unit, unit), unit)
        theirs = pl.ds(pl.multiple_of((2 * pair + 1 - side) * unit, unit), unit)
        left_ref[at : at + unit] = keep_ref[mine] + got_ref[mine].astype(F32)
        send_ref[at : at + unit] = (keep_ref[theirs] + got_ref[theirs].astype(F32)).astype(send_ref.dtype)
    mass = mass_in[:1] + get_mass(got_ref, rows)
    put_mass(send_ref, rows // 2, mass)
    mass_ref[...] = jnp.broadcast_to(mass, mass_ref.shape)


def last_kernel(
    groups, pack, keep_ref, got_ref, mass_in, loglik_in, image_out, occupancy_out, loglik_out,
    image_ref, occupancy_ref, loglik_ref, sems,
):
    loglik_ref[...] = loglik_in[0, : loglik_ref.shape[0]]
    copies = [pltpu.make_async_copy(loglik_ref, loglik_out, sems.at[0])]
    copies[0].start()
    block = image_ref.shape[1]
    rows = keep_ref.shape[0]
    total = keep_ref[...] + got_ref[:rows].astype(F32)
    for g in range(groups):
        for p in range(pack):
            image_ref[p * groups + g] = total[g * 8 + p * block : g * 8 + (p + 1) * block]
    copies.append(pltpu.make_async_copy(image_ref, image_out, sems.at[1]))
    copies[1].start()
    mass = mass_in[:1] + get_mass(got_ref, rows)
    occupancy_ref[...] = mass[0, : occupancy_ref.shape[0]]
    copies.append(pltpu.make_async_copy(occupancy_ref, occupancy_out, sems.at[2]))
    copies[2].start()
    for copy in copies:
        copy.wait()


def bits(count):
    return count.bit_length() - 1


def shards(n_dom, n_orient, particles, slices, freq_mask, slice_class, slice_orient, class_prior, orient_prior):
    count, crop, width = particles.shape
    share = slices.shape[0]
    lanes = share * TS
    block = crop // n_dom
    pack = 8 // block
    groups = share // pack
    vmem = pl.BlockSpec(memory_space=pltpu.VMEM)
    hbm = pl.BlockSpec(memory_space=pltpu.HBM)
    shape = jax.ShapeDtypeStruct
    params = pltpu.CompilerParams(vmem_limit_bytes=VMEM_LIMIT)
    order = [p * groups + g for g in range(groups) for p in range(pack)]
    tables = [jnp.asarray(t) for t in (*score_tables(crop, share), *back_tables(crop, share, order))]

    def call(kernel, outs, args, scratch, specs=None, outs_in=vmem, flops=0, name=None):
        return pl.pallas_call(
            kernel,
            out_shape=tuple(outs),
            in_specs=specs or [vmem] * len(args),
            out_specs=(outs_in,) * len(outs),
            scratch_shapes=scratch,
            compiler_params=params,
            cost_estimate=pl.CostEstimate(flops=flops, bytes_accessed=1 << 20, transcendentals=0),
            name=name,
        )(*args)

    def swap(value, r):
        core = parity(r, n_orient)
        pairs = [(d * n_orient + o, (d ^ core) * n_orient + (o ^ r)) for d in range(n_dom) for o in range(n_orient)]
        return lax.ppermute(value, ("dom", "orient"), pairs)

    flops = 2 * count * crop * share * width * 2 * lanes
    logits_shape, lse_shape = shape((count, TS, lanes), F32), shape((count, 128), F32)
    slices_shape = shape(slices.shape, F32)
    score_rows, score_columns, back_rows, back_columns = tables

    slots = [particles] + [swap(particles, r) for r in range(1, n_orient)]
    kept = (particles, freq_mask, *tables)
    logits, lse, first, second, bias, mine, mask, *tables = call(
        first_kernel,
        [logits_shape, lse_shape, slices_shape, slices_shape, shape((8, lanes), F32)]
        + [shape(value.shape, value.dtype) for value in kept],
        tuple(
            pltpu.with_memory_space_constraint(value, pltpu.HBM)
            for value in (
                slice_class, slice_orient, class_prior, orient_prior, particles, slices, freq_mask, score_rows,
                score_columns, back_rows, back_columns,
            )
        ),
        [
            pltpu.VMEM(slices.shape, slices.dtype),
            *[pltpu.SMEM(v.shape, v.dtype) for v in (slice_class, slice_orient, class_prior, orient_prior)],
            pltpu.SemaphoreType.DMA((11,)),
        ],
        specs=[hbm] * 11, flops=flops, name="first",
    )
    score_rows, score_columns, back_rows, back_columns = tables
    slots[0] = mine
    scored = [(logits, lse)] + [
        call(
            score_kernel, [logits_shape, lse_shape], (parts, first, second, bias, score_rows, score_columns), [],
            flops=flops, name="score",
        )
        for parts in slots[1:]
    ]
    terms = [[s[1]] for s in scored]
    for b in range(bits(n_orient)):
        sums = [functools.reduce(log_add, t) for t in terms]
        terms = [[sums[r], swap(sums[r ^ (1 << b)], 1 << b)] for r in range(n_orient)]

    rows = crop // block * groups * 8
    steps = bits(n_dom)

    def sent(step, height):
        dtype = F32 if step in (0, steps - 1) else BF16
        return shape((height + (8 if dtype == F32 else 16), width), dtype)

    mass_shape = shape((8, lanes), F32)
    turned = pltpu.VMEM((count, crop, width), F32)
    back_scratch = [turned, turned] + [pltpu.VMEM((count * TS, 2 * share * width), BF16)] * 2
    owns, = call(
        functools.partial(own_kernel, share, pack), [shape((count * rows, width), F32)],
        (*scored[0], slots[0], mask, back_rows, back_columns), back_scratch, flops=flops, name="own",
    )
    partial = ()
    for r in range(1, n_orient):
        partial = call(
            functools.partial(back_kernel, share, pack, r == 1, len(terms[r])),
            [shape((rows, width), F32), mass_shape],
            (scored[r][0], slots[r], mask, back_rows, back_columns, *terms[r], *partial),
            back_scratch, flops=flops, name="back",
        )
    keep, send, mass, loglik = call(
        functools.partial(last_back_kernel, share, len(terms[0])),
        [shape((rows // 2, width), F32), sent(0, rows // 2), shape((8, 128), F32), shape((8, 128), F32)],
        (*scored[0], owns, *partial, *terms[0]), [], flops=flops, name="last_back",
    )

    def exchange(value, b):
        step = 1 << b | 1
        return lax.ppermute(value, "dom", [(i, i ^ step) for i in range(n_dom)])

    for b in range(steps - 1):
        got = exchange(send, b)
        height = keep.shape[0] // 2
        keep, send, mass = call(
            functools.partial(halve_kernel, groups, b + 1),
            [shape((height, width), F32), sent(b + 1, height), shape((8, 128), F32)],
            (keep, got, mass), [], name="halve",
        )
    got = exchange(send, steps - 1)
    image, occupancy, loglik = call(
        functools.partial(last_kernel, groups, pack),
        [shape((share, block, width), F32), shape((share,), F32), shape((count,), F32)],
        (keep, got, mass, loglik),
        [
            pltpu.VMEM((share, block, width), F32), pltpu.VMEM((share,), F32), pltpu.VMEM((count,), F32),
            pltpu.SemaphoreType.DMA((3,)),
        ],
        outs_in=hbm, name="last",
    )
    return image, occupancy, loglik


def solution(mesh):
    placed = (P(("dom", "orient"), None, None), P("orient", None, None), P(), P(), P(), P(), P())
    return jax.shard_map(
        functools.partial(shards, mesh.shape["dom"], mesh.shape["orient"]),
        mesh=mesh,
        in_specs=placed,
        out_specs=(P("orient", "dom", None), P("orient"), P(("dom", "orient"))),
        check_vma=False,
    )
```

```python
import functools
import math

import jax
import jax.numpy as jnp
import ml_dtypes
import numpy as np
from jax import lax
from jax.experimental import pallas as pl
from jax.experimental.pallas import tpu as pltpu
from jax.sharding import PartitionSpec as P

TS = 16
F32 = jnp.float32
BF16 = jnp.bfloat16
VMEM_LIMIT = 24 * 1024 * 1024


def phase_tables(crop):
    freq = np.arange(crop, dtype=np.float64) - crop // 2
    offset = np.arange(TS, dtype=np.float64) - TS // 2
    angle = 2.0 * math.pi / crop * freq[:, None] * offset[None, :]
    return np.cos(angle).astype(np.float32), np.sin(angle).astype(np.float32)


def high_low(table):
    high = table.astype(ml_dtypes.bfloat16)
    low = (table - high.astype(np.float32)).astype(ml_dtypes.bfloat16)
    return high, low


def score_tables(crop, share):
    cosine, sine = phase_tables(crop)
    rows = np.zeros((share, 2, crop, 2, share, TS), np.float32)
    for j in range(share):
        rows[j, 0, :, 0, j] = cosine
        rows[j, 0, :, 1, j] = sine
        rows[j, 1, :, 0, j] = -sine
        rows[j, 1, :, 1, j] = cosine
    rows = rows.reshape(share * 2 * crop, 2 * share * TS).astype(ml_dtypes.bfloat16)
    high, low = high_low(np.concatenate([cosine.T, -sine.T], axis=1))
    columns = np.concatenate(
        [np.concatenate([high, high], axis=1), np.concatenate([low, np.zeros_like(low)], axis=1)], axis=0
    )
    return rows, columns


def back_tables(crop, share, order):
    cosine, sine = phase_tables(crop)
    rows = np.zeros((share, TS, 2, share, 2, crop), np.float32)
    for place, j in enumerate(order):
        rows[j, :, 0, place, 0] = cosine.T
        rows[j, :, 0, place, 1] = -sine.T
        rows[j, :, 1, place, 0] = -sine.T
        rows[j, :, 1, place, 1] = -cosine.T
    rows = rows.reshape(share * TS, 2 * share * 2 * crop).astype(ml_dtypes.bfloat16)
    high, low = high_low(np.concatenate([cosine, sine], axis=1))
    return rows, np.concatenate([high, high, low], axis=1)


def score_block(x_ref, first_ref, second_ref, bias, rows_ref, columns_ref, logits_ref, lse_ref):
    count, crop, width = x_ref.shape
    share = first_ref.shape[0]
    lanes = share * TS
    cross = []
    for i in range(count):
        x = x_ref[i].astype(F32)
        turned = pltpu.roll(x, width // 2, 1)
        terms = [(x * first_ref[j] + turned * second_ref[j]).astype(BF16) for j in range(share)]
        cross.append(jnp.concatenate(terms, axis=1))
    rowcorr = jnp.dot(jnp.concatenate(cross, axis=0), rows_ref[...], preferred_element_type=F32)
    high = rowcorr.astype(BF16)
    low = (rowcorr - high.astype(F32)).astype(BF16)
    stacked = jnp.concatenate(
        [
            jnp.concatenate(
                [part[i * crop : (i + 1) * crop, k * lanes : (k + 1) * lanes] for part in (high, low) for k in (0, 1)],
                axis=0,
            )
            for i in range(count)
        ],
        axis=1,
    )
    corr = jnp.dot(columns_ref[...], stacked, preferred_element_type=F32)
    corr = (corr[:TS] + corr[TS:]) * (1.0 / crop)
    logits = [corr[:, i * lanes : (i + 1) * lanes] + bias for i in range(count)]
    for i in range(count):
        logits_ref[i] = logits[i]
    tops = jnp.concatenate([jnp.max(value, axis=0, keepdims=True) for value in logits], axis=0)
    top = jnp.max(tops, axis=1, keepdims=True)
    sums = [jnp.sum(jnp.exp(logits[i] - top[i : i + 1]), axis=0, keepdims=True) for i in range(count)]
    total = jnp.sum(jnp.concatenate(sums, axis=0), axis=1, keepdims=True)
    lse_ref[...] = jnp.broadcast_to(top + jnp.log(total), lse_ref.shape)


def prepare_slices(s_ref, mask_ref, first, second):
    share, crop, width = s_ref.shape
    half = width // 2
    left = lax.broadcasted_iota(jnp.int32, (crop, width), 1) < half
    mask = mask_ref[...].astype(F32)
    mask = jnp.concatenate([mask, mask], axis=1)
    powers = []
    for j in range(share):
        s = s_ref[j].astype(F32) * mask
        turned = pltpu.roll(s, half, 1)
        first[j] = jnp.where(left, s, turned)
        second[j] = jnp.where(left, turned, -s)
        powers.append(jnp.sum(s * s, axis=0, keepdims=True))
    power = jnp.sum(jnp.concatenate(powers, axis=0), axis=1, keepdims=True) * (0.5 / crop)
    slot = lax.broadcasted_iota(jnp.int32, (1, share * TS), 1) // TS
    spread = jnp.zeros((1, share * TS), F32)
    for j in range(share):
        spread = jnp.where(slot == j, power[j : j + 1], spread)
    return spread


def first_kernel(*refs):
    sources, (logits_ref, lse_ref, first, second, bias_ref), kept = refs[:11], refs[11:16], refs[16:22]
    s_ref, class_ref, orient_ref, class_prior_ref, orient_prior_ref, sems = refs[22:]
    x_ref, mask_ref, rows_ref, columns_ref, back_rows_ref, back_columns_ref = kept
    targets = (
        class_ref, orient_ref, class_prior_ref, orient_prior_ref, x_ref, s_ref, mask_ref, rows_ref, columns_ref,
        back_rows_ref, back_columns_ref,
    )
    copies = [pltpu.make_async_copy(a, b, sems.at[k]) for k, (a, b) in enumerate(zip(sources, targets))]
    for copy in copies:
        copy.start()
    share = s_ref.shape[0]
    for copy in copies[:4]:
        copy.wait()
    slot = lax.broadcasted_iota(jnp.int32, (1, share * TS), 1) // TS
    prior = jnp.zeros((1, share * TS), F32)
    start = lax.axis_index("orient") * share
    for j in range(share):
        value = class_prior_ref[class_ref[start + j]] + orient_prior_ref[orient_ref[start + j]]
        prior = jnp.where(slot == j, value, prior)
    for copy in copies[4:7]:
        copy.wait()
    power = prepare_slices(s_ref, mask_ref, first, second)
    for copy in copies[7:9]:
        copy.wait()
    bias = prior - power
    bias_ref[...] = jnp.broadcast_to(bias, bias_ref.shape)
    score_block(x_ref, first, second, bias, rows_ref, columns_ref, logits_ref, lse_ref)
    for copy in copies[9:]:
        copy.wait()


def score_kernel(x_ref, first, second, bias_ref, rows_ref, columns_ref, logits_ref, lse_ref):
    score_block(x_ref, first, second, bias_ref[:1], rows_ref, columns_ref, logits_ref, lse_ref)


def log_add(a, b):
    top = jnp.maximum(a, b)
    return top + jnp.log(jnp.exp(a - top) + jnp.exp(b - top))


def parity(index, limit):
    total = index & 1
    for b in range(1, bits(limit)):
        total = total ^ ((index >> b) & 1)
    return total


def to_lanes(column):
    wide = jnp.broadcast_to(column, (column.shape[0], 128))
    row = lax.broadcasted_iota(jnp.int32, wide.shape, 0)
    lane = lax.broadcasted_iota(jnp.int32, wide.shape, 1)
    return jnp.sum(jnp.where(row == lane, wide, 0.0), axis=0, keepdims=True)


def put_mass(send_ref, at, mass):
    row = lax.broadcasted_iota(jnp.int32, (8, 128), 0)
    if send_ref.dtype == F32:
        send_ref[at : at + 8] = jnp.broadcast_to(mass, (8, 128))
    else:
        high = mass.astype(BF16).astype(F32)
        middle = (mass - high).astype(BF16).astype(F32)
        low = mass - high - middle
        terms = jnp.where(row == 0, high, jnp.where(row == 1, middle, jnp.where(row == 2, low, 0.0)))
        send_ref[at : at + 16] = jnp.concatenate([terms, jnp.zeros((8, 128), F32)], axis=0).astype(BF16)


def get_mass(got_ref, at):
    if got_ref.dtype == F32:
        return got_ref[at : at + 1]
    terms = got_ref[at : at + 16].astype(F32)
    return terms[0:1] + terms[1:2] + terms[2:3]


def double_particles(x_ref, doubled_re, doubled_im):
    count, crop, width = x_ref.shape
    left = lax.broadcasted_iota(jnp.int32, (crop, width), 1) < width // 2
    for i in range(count):
        x = x_ref[i].astype(F32)
        turned = pltpu.roll(x, width // 2, 1)
        doubled_re[i] = jnp.where(left, x, turned)
        doubled_im[i] = jnp.where(left, turned, x)


def put_spread(spread, high, low):
    rounded = spread.astype(BF16)
    high[...] = rounded
    low[...] = (spread - rounded.astype(F32)).astype(BF16)


def kernel_of(high, low, columns, k, group, wide):
    rows = slice(k * TS, (k + 1) * TS)
    here = slice(group * wide, (group + 1) * wide)
    there = slice(high.shape[1] // 2 + group * wide, high.shape[1] // 2 + (group + 1) * wide)
    a, b = high[rows, here], high[rows, there]
    terms = jnp.concatenate([a, b, low[rows, here], low[rows, there], a, b], axis=0)
    return jnp.dot(columns, terms, preferred_element_type=F32)


def put_images(re, im, mask, odd, pack, group, groups, out_ref, at):
    crop, width = mask.shape
    half = width // 2
    signed = jnp.where(lax.broadcasted_iota(jnp.int32, (1, width), 1) < half, -mask, mask)
    images = []
    for p in range(pack):
        here = slice(p * width, (p + 1) * width)
        images.append(re[:, here] * mask + pltpu.roll(im[:, here], half, 1) * signed)
    block = 8 // pack
    tiles = [jnp.concatenate([image[r : r + block] for image in images], axis=0) for r in range(0, crop, block)]
    pairs = len(tiles) // 2
    for pair in range(pairs):
        even, other = tiles[2 * pair], tiles[2 * pair + 1]
        if parity(pair, crop):
            even, other = other, even
        kept, given = at + (pair * groups + group) * 8, at + ((pairs + pair) * groups + group) * 8
        out_ref[kept : kept + 8] = jnp.where(odd == 1, other, even)
        out_ref[given : given + 8] = jnp.where(odd == 1, even, other)


def twice_mask(mask_ref):
    mask = mask_ref[...].astype(F32)
    return jnp.concatenate([mask, mask], axis=1)


def own_kernel(
    share, pack, logits_ref, lse_ref, x_ref, mask_ref, rows_ref, columns_ref, out_ref, doubled_re, doubled_im, high, low
):
    count, crop, width = x_ref.shape
    double_particles(x_ref, doubled_re, doubled_im)
    weights = jnp.concatenate([jnp.exp(logits_ref[i] - lse_ref[i : i + 1, :]) for i in range(count)], axis=0)
    rounded = weights.astype(BF16)
    rest = (weights - rounded.astype(F32)).astype(BF16)
    rows = rows_ref[...]
    put_spread(
        jnp.dot(rounded, rows, preferred_element_type=F32) + jnp.dot(rest, rows, preferred_element_type=F32), high, low
    )
    columns = columns_ref[...]
    mask = twice_mask(mask_ref)
    odd = parity(lax.axis_index("dom"), crop * pack // 8)
    height = crop * share
    for group in range(share // pack):
        for k in range(count):
            kernel = kernel_of(high, low, columns, k, group, pack * width)
            re = kernel * jnp.concatenate([doubled_re[k]] * pack, axis=1)
            im = kernel * jnp.concatenate([doubled_im[k]] * pack, axis=1)
            put_images(re, im, mask, odd, pack, group, share // pack, out_ref, k * height)


def back_kernel(share, pack, start, n_lse, *refs):
    refs = list(refs)
    logits_ref, x_ref, mask_ref, rows_ref, columns_ref = refs[:5]
    lse_refs = refs[5 : 5 + n_lse]
    del refs[: 5 + n_lse]
    if not start:
        out_in, mass_in = refs[:2]
        del refs[:2]
    out_ref, mass_ref, doubled_re, doubled_im, high, low = refs
    count, crop, width = x_ref.shape
    loglik = functools.reduce(log_add, [ref[...] for ref in lse_refs])
    double_particles(x_ref, doubled_re, doubled_im)
    mass = jnp.zeros((TS, share * TS), F32)
    weights = []
    for i in range(count):
        weight = jnp.exp(logits_ref[i] - loglik[i : i + 1, :]).astype(BF16)
        mass = mass + weight.astype(F32)
        weights.append(weight)
    mass = jnp.sum(mass, axis=0, keepdims=True)
    if not start:
        mass = mass + mass_in[:1]
    mass_ref[...] = jnp.broadcast_to(mass, mass_ref.shape)
    put_spread(jnp.dot(jnp.concatenate(weights, axis=0), rows_ref[...], preferred_element_type=F32), high, low)
    wide = pack * width
    columns = columns_ref[...]
    mask = twice_mask(mask_ref)
    odd = parity(lax.axis_index("dom"), crop * pack // 8)
    for group in range(share // pack):
        re = jnp.zeros((crop, wide), F32)
        im = jnp.zeros((crop, wide), F32)
        for k in range(count):
            kernel = kernel_of(high, low, columns, k, group, wide)
            re = re + kernel * jnp.concatenate([doubled_re[k]] * pack, axis=1)
            im = im + kernel * jnp.concatenate([doubled_im[k]] * pack, axis=1)
        put_images(re, im, mask, odd, pack, group, share // pack, out_ref, 0)
    if not start:
        out_ref[...] = out_ref[...] + out_in[...]


def last_back_kernel(share, n_lse, logits_ref, lse_ref, own_ref, sum_ref, mass_in, *refs):
    lse_refs = refs[:n_lse]
    keep_ref, send_ref, mass_ref, loglik_ref = refs[n_lse:]
    count = logits_ref.shape[0]
    loglik = functools.reduce(log_add, [ref[...] for ref in lse_refs])
    factor = jnp.exp(lse_ref[...] - loglik)
    mass = jnp.zeros((TS, share * TS), F32)
    for i in range(count):
        mass = mass + jnp.exp(logits_ref[i] - loglik[i : i + 1, :]).astype(BF16).astype(F32)
    mass = jnp.sum(mass, axis=0, keepdims=True) + mass_in[:1]
    row = lax.broadcasted_iota(jnp.int32, (share, share * TS), 0)
    lane = lax.broadcasted_iota(jnp.int32, (share, share * TS), 1)
    mass = to_lanes(jnp.sum(jnp.where(row == lane // TS, mass, 0.0), axis=1, keepdims=True))
    height = sum_ref.shape[0]
    half = height // 2
    factors = [jnp.broadcast_to(factor[i : i + 1, :], (8, factor.shape[1])) for i in range(count)]
    for at in range(0, height, 8):
        total = sum_ref[at : at + 8]
        for i in range(count):
            total = total + own_ref[i * height + at : i * height + at + 8] * factors[i]
        if at < half:
            keep_ref[at : at + 8] = total
        else:
            send_ref[at - half : at - half + 8] = total
    put_mass(send_ref, half, mass)
    loglik_ref[...] = jnp.broadcast_to(to_lanes(loglik[:, :1]), loglik_ref.shape)
    mass_ref[...] = jnp.broadcast_to(mass, mass_ref.shape)


def quarter_kernel(unit, keep_ref, got_ref, mass_in, left_ref, *refs):
    sends, mass_ref = refs[:-1], refs[-1]
    rows = keep_ref.shape[0]
    own = (lax.axis_index("dom") >> 1) & 3
    mass = mass_in[:1] + get_mass(got_ref, rows)
    for turn, out_ref in enumerate((left_ref, *sends)):
        for rest in range(rows // unit // 4):
            at = rest * unit
            here = pl.ds(pl.multiple_of((4 * rest + (own ^ turn)) * unit, unit), unit)
            out_ref[at : at + unit] = (keep_ref[here] + got_ref[here].astype(F32)).astype(out_ref.dtype)
        if turn:
            put_mass(out_ref, rows // 4, mass)
    mass_ref[...] = jnp.broadcast_to(mass, mass_ref.shape)


def halve_kernel(unit, bit, keep_ref, mass_in, *refs):
    gots, (left_ref, send_ref, mass_ref) = refs[:-3], refs[-3:]
    rows = keep_ref.shape[0]
    side = (lax.axis_index("dom") >> bit) & 1
    mass = mass_in[:1]
    for got_ref in gots:
        mass = mass + get_mass(got_ref, rows)
    for pair in range(rows // unit // 2):
        at = pair * unit
        for half, out_ref in ((side, left_ref), (1 - side, send_ref)):
            here = pl.ds(pl.multiple_of((2 * pair + half) * unit, unit), unit)
            total = keep_ref[here]
            for got_ref in gots:
                total = total + got_ref[here].astype(F32)
            out_ref[at : at + unit] = total.astype(out_ref.dtype)
    put_mass(send_ref, rows // 2, mass)
    mass_ref[...] = jnp.broadcast_to(mass, mass_ref.shape)


def last_kernel(
    groups, pack, keep_ref, got_ref, mass_in, loglik_in, image_out, occupancy_out, loglik_out,
    image_ref, occupancy_ref, loglik_ref, sems,
):
    loglik_ref[...] = loglik_in[0, : loglik_ref.shape[0]]
    copies = [pltpu.make_async_copy(loglik_ref, loglik_out, sems.at[0])]
    copies[0].start()
    block = image_ref.shape[1]
    rows = keep_ref.shape[0]
    total = keep_ref[...] + got_ref[:rows].astype(F32)
    for g in range(groups):
        for p in range(pack):
            image_ref[p * groups + g] = total[g * 8 + p * block : g * 8 + (p + 1) * block]
    copies.append(pltpu.make_async_copy(image_ref, image_out, sems.at[1]))
    copies[1].start()
    mass = mass_in[:1] + get_mass(got_ref, rows)
    occupancy_ref[...] = mass[0, : occupancy_ref.shape[0]]
    copies.append(pltpu.make_async_copy(occupancy_ref, occupancy_out, sems.at[2]))
    copies[2].start()
    for copy in copies:
        copy.wait()


def bits(count):
    return count.bit_length() - 1


def shards(n_dom, n_orient, particles, slices, freq_mask, slice_class, slice_orient, class_prior, orient_prior):
    count, crop, width = particles.shape
    share = slices.shape[0]
    lanes = share * TS
    block = crop // n_dom
    pack = 8 // block
    groups = share // pack
    vmem = pl.BlockSpec(memory_space=pltpu.VMEM)
    hbm = pl.BlockSpec(memory_space=pltpu.HBM)
    shape = jax.ShapeDtypeStruct
    params = pltpu.CompilerParams(vmem_limit_bytes=VMEM_LIMIT)
    order = [p * groups + g for g in range(groups) for p in range(pack)]
    tables = [jnp.asarray(t) for t in (*score_tables(crop, share), *back_tables(crop, share, order))]

    def call(kernel, outs, args, scratch, specs=None, outs_in=vmem, flops=0, name=None):
        return pl.pallas_call(
            kernel,
            out_shape=tuple(outs),
            in_specs=specs or [vmem] * len(args),
            out_specs=(outs_in,) * len(outs),
            scratch_shapes=scratch,
            compiler_params=params,
            cost_estimate=pl.CostEstimate(flops=flops, bytes_accessed=1 << 20, transcendentals=0),
            name=name,
        )(*args)

    def swap(value, r):
        core = parity(r, n_orient)
        pairs = [(d * n_orient + o, (d ^ core) * n_orient + (o ^ r)) for d in range(n_dom) for o in range(n_orient)]
        return lax.ppermute(value, ("dom", "orient"), pairs)

    flops = 2 * count * crop * share * width * 2 * lanes
    logits_shape, lse_shape = shape((count, TS, lanes), F32), shape((count, 128), F32)
    slices_shape = shape(slices.shape, F32)
    score_rows, score_columns, back_rows, back_columns = tables

    slots = [particles] + [swap(particles, r) for r in range(1, n_orient)]
    kept = (particles, freq_mask, *tables)
    logits, lse, first, second, bias, mine, mask, *tables = call(
        first_kernel,
        [logits_shape, lse_shape, slices_shape, slices_shape, shape((8, lanes), F32)]
        + [shape(value.shape, value.dtype) for value in kept],
        tuple(
            pltpu.with_memory_space_constraint(value, pltpu.HBM)
            for value in (
                slice_class, slice_orient, class_prior, orient_prior, particles, slices, freq_mask, score_rows,
                score_columns, back_rows, back_columns,
            )
        ),
        [
            pltpu.VMEM(slices.shape, slices.dtype),
            *[pltpu.SMEM(v.shape, v.dtype) for v in (slice_class, slice_orient, class_prior, orient_prior)],
            pltpu.SemaphoreType.DMA((11,)),
        ],
        specs=[hbm] * 11, flops=flops, name="first",
    )
    score_rows, score_columns, back_rows, back_columns = tables
    slots[0] = mine
    scored = [(logits, lse)] + [
        call(
            score_kernel, [logits_shape, lse_shape], (parts, first, second, bias, score_rows, score_columns), [],
            flops=flops, name="score",
        )
        for parts in slots[1:]
    ]
    terms = [[s[1]] for s in scored]
    for b in range(bits(n_orient)):
        sums = [functools.reduce(log_add, t) for t in terms]
        terms = [[sums[r], swap(sums[r ^ (1 << b)], 1 << b)] for r in range(n_orient)]

    rows = crop // block * groups * 8
    steps = bits(n_dom)

    def sent(step, height):
        dtype = F32 if step in (0, steps - 1) else BF16
        return shape((height + (8 if dtype == F32 else 16), width), dtype)

    mass_shape = shape((8, lanes), F32)
    turned = pltpu.VMEM((count, crop, width), F32)
    back_scratch = [turned, turned] + [pltpu.VMEM((count * TS, 2 * share * width), BF16)] * 2
    owns, = call(
        functools.partial(own_kernel, share, pack), [shape((count * rows, width), F32)],
        (*scored[0], slots[0], mask, back_rows, back_columns), back_scratch, flops=flops, name="own",
    )
    partial = ()
    for r in range(1, n_orient):
        partial = call(
            functools.partial(back_kernel, share, pack, r == 1, len(terms[r])),
            [shape((rows, width), F32), mass_shape],
            (scored[r][0], slots[r], mask, back_rows, back_columns, *terms[r], *partial),
            back_scratch, flops=flops, name="back",
        )
    keep, send, mass, loglik = call(
        functools.partial(last_back_kernel, share, len(terms[0])),
        [shape((rows // 2, width), F32), sent(0, rows // 2), shape((8, 128), F32), shape((8, 128), F32)],
        (*scored[0], owns, *partial, *terms[0]), [], flops=flops, name="last_back",
    )

    def exchange(value, turned):
        step = turned | parity(turned >> 1, n_dom)
        return lax.ppermute(value, "dom", [(i, i ^ step) for i in range(n_dom)])

    got = exchange(send, 1)
    height = keep.shape[0] // 4
    keep, *sends, mass = call(
        functools.partial(quarter_kernel, groups * 8),
        [shape((height, width), F32)] + [sent(1, height)] * 3 + [shape((8, 128), F32)],
        (keep, got, mass), [], name="quarter",
    )
    gots = [exchange(sends[turn - 1], turn << 1) for turn in (1, 3, 2)]
    for b in range(3, steps):
        height = keep.shape[0] // 2
        keep, send, mass = call(
            functools.partial(halve_kernel, groups * 8, b),
            [shape((height, width), F32), sent(b, height), shape((8, 128), F32)],
            (keep, mass, *gots), [], name="halve",
        )
        gots = [exchange(send, 1 << b)]
    got, = gots
    image, occupancy, loglik = call(
        functools.partial(last_kernel, groups, pack),
        [shape((share, block, width), F32), shape((share,), F32), shape((count,), F32)],
        (keep, got, mass, loglik),
        [
            pltpu.VMEM((share, block, width), F32), pltpu.VMEM((share,), F32), pltpu.VMEM((count,), F32),
            pltpu.SemaphoreType.DMA((3,)),
        ],
        outs_in=hbm, name="last",
    )
    return image, occupancy, loglik


def solution(mesh):
    placed = (P(("dom", "orient"), None, None), P("orient", None, None), P(), P(), P(), P(), P())
    return jax.shard_map(
        functools.partial(shards, mesh.shape["dom"], mesh.shape["orient"]),
        mesh=mesh,
        in_specs=placed,
        out_specs=(P("orient", "dom", None), P("orient"), P(("dom", "orient"))),
        check_vma=False,
    )
```

```python
import functools
import math

import jax
import jax.numpy as jnp
import ml_dtypes
import numpy as np
from jax import lax
from jax.experimental import pallas as pl
from jax.experimental.pallas import tpu as pltpu
from jax.sharding import PartitionSpec as P

TS = 16
F32 = jnp.float32
BF16 = jnp.bfloat16
VMEM_LIMIT = 24 * 1024 * 1024


def phase_tables(crop):
    freq = np.arange(crop, dtype=np.float64) - crop // 2
    offset = np.arange(TS, dtype=np.float64) - TS // 2
    angle = 2.0 * math.pi / crop * freq[:, None] * offset[None, :]
    return np.cos(angle).astype(np.float32), np.sin(angle).astype(np.float32)


def high_low(table):
    high = table.astype(ml_dtypes.bfloat16)
    low = (table - high.astype(np.float32)).astype(ml_dtypes.bfloat16)
    return high, low


def score_tables(crop, share):
    cosine, sine = phase_tables(crop)
    rows = np.zeros((share, 2, crop, 2, share, TS), np.float32)
    for j in range(share):
        rows[j, 0, :, 0, j] = cosine
        rows[j, 0, :, 1, j] = sine
        rows[j, 1, :, 0, j] = -sine
        rows[j, 1, :, 1, j] = cosine
    rows = rows.reshape(share * 2 * crop, 2 * share * TS).astype(ml_dtypes.bfloat16)
    high, low = high_low(np.concatenate([cosine.T, -sine.T], axis=1))
    columns = np.concatenate(
        [np.concatenate([high, high], axis=1), np.concatenate([low, np.zeros_like(low)], axis=1)], axis=0
    )
    return rows, columns


def back_tables(crop, share, order):
    cosine, sine = phase_tables(crop)
    rows = np.zeros((share, TS, 2, share, 2, crop), np.float32)
    for place, j in enumerate(order):
        rows[j, :, 0, place, 0] = cosine.T
        rows[j, :, 0, place, 1] = -sine.T
        rows[j, :, 1, place, 0] = -sine.T
        rows[j, :, 1, place, 1] = -cosine.T
    rows = rows.reshape(share * TS, 2 * share * 2 * crop).astype(ml_dtypes.bfloat16)
    high, low = high_low(np.concatenate([cosine, sine], axis=1))
    return rows, np.concatenate([high, high, low], axis=1)


def score_block(x_ref, first_ref, second_ref, bias, rows_ref, columns_ref, logits_ref, lse_ref):
    count, crop, width = x_ref.shape
    share = first_ref.shape[0]
    lanes = share * TS
    cross = []
    for i in range(count):
        x = x_ref[i].astype(F32)
        turned = pltpu.roll(x, width // 2, 1)
        terms = [(x * first_ref[j] + turned * second_ref[j]).astype(BF16) for j in range(share)]
        cross.append(jnp.concatenate(terms, axis=1))
    rowcorr = jnp.dot(jnp.concatenate(cross, axis=0), rows_ref[...], preferred_element_type=F32)
    high = rowcorr.astype(BF16)
    low = (rowcorr - high.astype(F32)).astype(BF16)
    stacked = jnp.concatenate(
        [
            jnp.concatenate(
                [part[i * crop : (i + 1) * crop, k * lanes : (k + 1) * lanes] for part in (high, low) for k in (0, 1)],
                axis=0,
            )
            for i in range(count)
        ],
        axis=1,
    )
    corr = jnp.dot(columns_ref[...], stacked, preferred_element_type=F32)
    corr = (corr[:TS] + corr[TS:]) * (1.0 / crop)
    logits = [corr[:, i * lanes : (i + 1) * lanes] + bias for i in range(count)]
    for i in range(count):
        logits_ref[i] = logits[i]
    tops = jnp.concatenate([jnp.max(value, axis=0, keepdims=True) for value in logits], axis=0)
    top = jnp.max(tops, axis=1, keepdims=True)
    sums = [jnp.sum(jnp.exp(logits[i] - top[i : i + 1]), axis=0, keepdims=True) for i in range(count)]
    total = jnp.sum(jnp.concatenate(sums, axis=0), axis=1, keepdims=True)
    lse_ref[...] = jnp.broadcast_to(top + jnp.log(total), lse_ref.shape)


def prepare_slices(s_ref, mask_ref, first, second):
    share, crop, width = s_ref.shape
    half = width // 2
    left = lax.broadcasted_iota(jnp.int32, (crop, width), 1) < half
    mask = mask_ref[...].astype(F32)
    mask = jnp.concatenate([mask, mask], axis=1)
    powers = []
    for j in range(share):
        s = s_ref[j].astype(F32) * mask
        turned = pltpu.roll(s, half, 1)
        first[j] = jnp.where(left, s, turned)
        second[j] = jnp.where(left, turned, -s)
        powers.append(jnp.sum(s * s, axis=0, keepdims=True))
    power = jnp.sum(jnp.concatenate(powers, axis=0), axis=1, keepdims=True) * (0.5 / crop)
    slot = lax.broadcasted_iota(jnp.int32, (1, share * TS), 1) // TS
    spread = jnp.zeros((1, share * TS), F32)
    for j in range(share):
        spread = jnp.where(slot == j, power[j : j + 1], spread)
    return spread


def first_kernel(*refs):
    sources, (logits_ref, lse_ref, first, second, bias_ref), kept = refs[:11], refs[11:16], refs[16:22]
    s_ref, class_ref, orient_ref, class_prior_ref, orient_prior_ref, sems = refs[22:]
    x_ref, mask_ref, rows_ref, columns_ref, back_rows_ref, back_columns_ref = kept
    targets = (
        class_ref, orient_ref, class_prior_ref, orient_prior_ref, x_ref, s_ref, mask_ref, rows_ref, columns_ref,
        back_rows_ref, back_columns_ref,
    )
    copies = [pltpu.make_async_copy(a, b, sems.at[k]) for k, (a, b) in enumerate(zip(sources, targets))]
    for copy in copies:
        copy.start()
    share = s_ref.shape[0]
    for copy in copies[:4]:
        copy.wait()
    slot = lax.broadcasted_iota(jnp.int32, (1, share * TS), 1) // TS
    prior = jnp.zeros((1, share * TS), F32)
    start = lax.axis_index("orient") * share
    for j in range(share):
        value = class_prior_ref[class_ref[start + j]] + orient_prior_ref[orient_ref[start + j]]
        prior = jnp.where(slot == j, value, prior)
    for copy in copies[4:7]:
        copy.wait()
    power = prepare_slices(s_ref, mask_ref, first, second)
    for copy in copies[7:9]:
        copy.wait()
    bias = prior - power
    bias_ref[...] = jnp.broadcast_to(bias, bias_ref.shape)
    score_block(x_ref, first, second, bias, rows_ref, columns_ref, logits_ref, lse_ref)
    for copy in copies[9:]:
        copy.wait()


def score_kernel(x_ref, first, second, bias_ref, rows_ref, columns_ref, logits_ref, lse_ref):
    score_block(x_ref, first, second, bias_ref[:1], rows_ref, columns_ref, logits_ref, lse_ref)


def log_add(a, b):
    top = jnp.maximum(a, b)
    return top + jnp.log(jnp.exp(a - top) + jnp.exp(b - top))


def parity(index, limit):
    total = index & 1
    for b in range(1, bits(limit)):
        total = total ^ ((index >> b) & 1)
    return total


def to_lanes(column):
    wide = jnp.broadcast_to(column, (column.shape[0], 128))
    row = lax.broadcasted_iota(jnp.int32, wide.shape, 0)
    lane = lax.broadcasted_iota(jnp.int32, wide.shape, 1)
    return jnp.sum(jnp.where(row == lane, wide, 0.0), axis=0, keepdims=True)


def put_mass(send_ref, at, mass):
    row = lax.broadcasted_iota(jnp.int32, (8, 128), 0)
    if send_ref.dtype == F32:
        send_ref[at : at + 8] = jnp.broadcast_to(mass, (8, 128))
    else:
        high = mass.astype(BF16).astype(F32)
        middle = (mass - high).astype(BF16).astype(F32)
        low = mass - high - middle
        terms = jnp.where(row == 0, high, jnp.where(row == 1, middle, jnp.where(row == 2, low, 0.0)))
        send_ref[at : at + 16] = jnp.concatenate([terms, jnp.zeros((8, 128), F32)], axis=0).astype(BF16)


def get_mass(got_ref, at):
    if got_ref.dtype == F32:
        return got_ref[at : at + 1]
    terms = got_ref[at : at + 16].astype(F32)
    return terms[0:1] + terms[1:2] + terms[2:3]


def double_particles(x_ref, doubled_re, doubled_im):
    count, crop, width = x_ref.shape
    left = lax.broadcasted_iota(jnp.int32, (crop, width), 1) < width // 2
    for i in range(count):
        x = x_ref[i].astype(F32)
        turned = pltpu.roll(x, width // 2, 1)
        doubled_re[i] = jnp.where(left, x, turned)
        doubled_im[i] = jnp.where(left, turned, x)


def put_spread(spread, high, low):
    rounded = spread.astype(BF16)
    high[...] = rounded
    low[...] = (spread - rounded.astype(F32)).astype(BF16)


def kernel_of(high, low, columns, k, group, wide):
    rows = slice(k * TS, (k + 1) * TS)
    here = slice(group * wide, (group + 1) * wide)
    there = slice(high.shape[1] // 2 + group * wide, high.shape[1] // 2 + (group + 1) * wide)
    a, b = high[rows, here], high[rows, there]
    terms = jnp.concatenate([a, b, low[rows, here], low[rows, there], a, b], axis=0)
    return jnp.dot(columns, terms, preferred_element_type=F32)


def put_images(re, im, mask, odd, pack, group, groups, out_ref, at):
    crop, width = mask.shape
    half = width // 2
    signed = jnp.where(lax.broadcasted_iota(jnp.int32, (1, width), 1) < half, -mask, mask)
    images = []
    for p in range(pack):
        here = slice(p * width, (p + 1) * width)
        images.append(re[:, here] * mask + pltpu.roll(im[:, here], half, 1) * signed)
    block = 8 // pack
    tiles = [jnp.concatenate([image[r : r + block] for image in images], axis=0) for r in range(0, crop, block)]
    pairs = len(tiles) // 2
    for pair in range(pairs):
        even, other = tiles[2 * pair], tiles[2 * pair + 1]
        if parity(pair, crop):
            even, other = other, even
        kept, given = at + (pair * groups + group) * 8, at + ((pairs + pair) * groups + group) * 8
        out_ref[kept : kept + 8] = jnp.where(odd == 1, other, even)
        out_ref[given : given + 8] = jnp.where(odd == 1, even, other)


def twice_mask(mask_ref):
    mask = mask_ref[...].astype(F32)
    return jnp.concatenate([mask, mask], axis=1)


def own_kernel(
    share, pack, logits_ref, lse_ref, x_ref, mask_ref, rows_ref, columns_ref, out_ref, doubled_re, doubled_im, high, low
):
    count, crop, width = x_ref.shape
    double_particles(x_ref, doubled_re, doubled_im)
    weights = jnp.concatenate([jnp.exp(logits_ref[i] - lse_ref[i : i + 1, :]) for i in range(count)], axis=0)
    rounded = weights.astype(BF16)
    rest = (weights - rounded.astype(F32)).astype(BF16)
    rows = rows_ref[...]
    put_spread(
        jnp.dot(rounded, rows, preferred_element_type=F32) + jnp.dot(rest, rows, preferred_element_type=F32), high, low
    )
    columns = columns_ref[...]
    mask = twice_mask(mask_ref)
    odd = parity(lax.axis_index("dom"), crop * pack // 8)
    height = crop * share
    for group in range(share // pack):
        for k in range(count):
            kernel = kernel_of(high, low, columns, k, group, pack * width)
            re = kernel * jnp.concatenate([doubled_re[k]] * pack, axis=1)
            im = kernel * jnp.concatenate([doubled_im[k]] * pack, axis=1)
            put_images(re, im, mask, odd, pack, group, share // pack, out_ref, k * height)


def back_kernel(share, pack, start, n_lse, *refs):
    refs = list(refs)
    logits_ref, x_ref, mask_ref, rows_ref, columns_ref = refs[:5]
    lse_refs = refs[5 : 5 + n_lse]
    del refs[: 5 + n_lse]
    if not start:
        out_in, mass_in = refs[:2]
        del refs[:2]
    out_ref, mass_ref, doubled_re, doubled_im, high, low = refs
    count, crop, width = x_ref.shape
    loglik = functools.reduce(log_add, [ref[...] for ref in lse_refs])
    double_particles(x_ref, doubled_re, doubled_im)
    mass = jnp.zeros((TS, share * TS), F32)
    weights = []
    for i in range(count):
        weight = jnp.exp(logits_ref[i] - loglik[i : i + 1, :]).astype(BF16)
        mass = mass + weight.astype(F32)
        weights.append(weight)
    mass = jnp.sum(mass, axis=0, keepdims=True)
    if not start:
        mass = mass + mass_in[:1]
    mass_ref[...] = jnp.broadcast_to(mass, mass_ref.shape)
    put_spread(jnp.dot(jnp.concatenate(weights, axis=0), rows_ref[...], preferred_element_type=F32), high, low)
    wide = pack * width
    columns = columns_ref[...]
    mask = twice_mask(mask_ref)
    odd = parity(lax.axis_index("dom"), crop * pack // 8)
    for group in range(share // pack):
        re = jnp.zeros((crop, wide), F32)
        im = jnp.zeros((crop, wide), F32)
        for k in range(count):
            kernel = kernel_of(high, low, columns, k, group, wide)
            re = re + kernel * jnp.concatenate([doubled_re[k]] * pack, axis=1)
            im = im + kernel * jnp.concatenate([doubled_im[k]] * pack, axis=1)
        put_images(re, im, mask, odd, pack, group, share // pack, out_ref, 0)
    if not start:
        out_ref[...] = out_ref[...] + out_in[...]


def last_back_kernel(share, n_lse, logits_ref, lse_ref, own_ref, sum_ref, mass_in, *refs):
    lse_refs = refs[:n_lse]
    keep_ref, send_ref, mass_ref, loglik_ref = refs[n_lse:]
    count = logits_ref.shape[0]
    loglik = functools.reduce(log_add, [ref[...] for ref in lse_refs])
    factor = jnp.exp(lse_ref[...] - loglik)
    mass = jnp.zeros((TS, share * TS), F32)
    for i in range(count):
        mass = mass + jnp.exp(logits_ref[i] - loglik[i : i + 1, :]).astype(BF16).astype(F32)
    mass = jnp.sum(mass, axis=0, keepdims=True) + mass_in[:1]
    row = lax.broadcasted_iota(jnp.int32, (share, share * TS), 0)
    lane = lax.broadcasted_iota(jnp.int32, (share, share * TS), 1)
    mass = to_lanes(jnp.sum(jnp.where(row == lane // TS, mass, 0.0), axis=1, keepdims=True))
    height = sum_ref.shape[0]
    half = height // 2
    factors = [jnp.broadcast_to(factor[i : i + 1, :], (16, factor.shape[1])) for i in range(count)]
    for at in range(0, height, 16):
        total = sum_ref[at : at + 16]
        for i in range(count):
            total = total + own_ref[i * height + at : i * height + at + 16] * factors[i]
        if at < half:
            keep_ref[at : at + 16] = total
        else:
            send_ref[at - half : at - half + 16] = total.astype(send_ref.dtype)
    put_mass(send_ref, half, mass)
    loglik_ref[...] = jnp.broadcast_to(to_lanes(loglik[:, :1]), loglik_ref.shape)
    mass_ref[...] = jnp.broadcast_to(mass, mass_ref.shape)


def quarter_kernel(unit, keep_ref, got_ref, mass_in, left_ref, *refs):
    sends, mass_ref = refs[:-1], refs[-1]
    rows = keep_ref.shape[0]
    own = (lax.axis_index("dom") >> 1) & 3
    mass = mass_in[:1] + get_mass(got_ref, rows)
    for turn, out_ref in enumerate((left_ref, *sends)):
        for rest in range(rows // unit // 4):
            at = rest * unit
            here = pl.ds(pl.multiple_of((4 * rest + (own ^ turn)) * unit, unit), unit)
            out_ref[at : at + unit] = (keep_ref[here] + got_ref[here].astype(F32)).astype(out_ref.dtype)
        if turn:
            put_mass(out_ref, rows // 4, mass)
    mass_ref[...] = jnp.broadcast_to(mass, mass_ref.shape)


def halve_kernel(unit, bit, keep_ref, mass_in, *refs):
    gots, (left_ref, send_ref, mass_ref) = refs[:-3], refs[-3:]
    rows = keep_ref.shape[0]
    side = (lax.axis_index("dom") >> bit) & 1
    mass = mass_in[:1]
    for got_ref in gots:
        mass = mass + get_mass(got_ref, rows)
    for pair in range(rows // unit // 2):
        at = pair * unit
        for half, out_ref in ((side, left_ref), (1 - side, send_ref)):
            here = pl.ds(pl.multiple_of((2 * pair + half) * unit, unit), unit)
            total = keep_ref[here]
            for got_ref in gots:
                total = total + got_ref[here].astype(F32)
            out_ref[at : at + unit] = total.astype(out_ref.dtype)
    put_mass(send_ref, rows // 2, mass)
    mass_ref[...] = jnp.broadcast_to(mass, mass_ref.shape)


def last_kernel(
    groups, pack, keep_ref, got_ref, mass_in, loglik_in, image_out, occupancy_out, loglik_out,
    image_ref, occupancy_ref, loglik_ref, sems,
):
    loglik_ref[...] = loglik_in[0, : loglik_ref.shape[0]]
    copies = [pltpu.make_async_copy(loglik_ref, loglik_out, sems.at[0])]
    copies[0].start()
    block = image_ref.shape[1]
    rows = keep_ref.shape[0]
    total = keep_ref[...] + got_ref[:rows].astype(F32)
    for g in range(groups):
        for p in range(pack):
            image_ref[p * groups + g] = total[g * 8 + p * block : g * 8 + (p + 1) * block]
    copies.append(pltpu.make_async_copy(image_ref, image_out, sems.at[1]))
    copies[1].start()
    mass = mass_in[:1] + get_mass(got_ref, rows)
    occupancy_ref[...] = mass[0, : occupancy_ref.shape[0]]
    copies.append(pltpu.make_async_copy(occupancy_ref, occupancy_out, sems.at[2]))
    copies[2].start()
    for copy in copies:
        copy.wait()


def bits(count):
    return count.bit_length() - 1


def shards(n_dom, n_orient, particles, slices, freq_mask, slice_class, slice_orient, class_prior, orient_prior):
    count, crop, width = particles.shape
    share = slices.shape[0]
    lanes = share * TS
    block = crop // n_dom
    pack = 8 // block
    groups = share // pack
    vmem = pl.BlockSpec(memory_space=pltpu.VMEM)
    hbm = pl.BlockSpec(memory_space=pltpu.HBM)
    shape = jax.ShapeDtypeStruct
    params = pltpu.CompilerParams(vmem_limit_bytes=VMEM_LIMIT)
    order = [p * groups + g for g in range(groups) for p in range(pack)]
    tables = [jnp.asarray(t) for t in (*score_tables(crop, share), *back_tables(crop, share, order))]

    def call(kernel, outs, args, scratch, specs=None, outs_in=vmem, flops=0, name=None):
        return pl.pallas_call(
            kernel,
            out_shape=tuple(outs),
            in_specs=specs or [vmem] * len(args),
            out_specs=(outs_in,) * len(outs),
            scratch_shapes=scratch,
            compiler_params=params,
            cost_estimate=pl.CostEstimate(flops=flops, bytes_accessed=1 << 20, transcendentals=0),
            name=name,
        )(*args)

    def swap(value, r):
        core = parity(r, n_orient)
        pairs = [(d * n_orient + o, (d ^ core) * n_orient + (o ^ r)) for d in range(n_dom) for o in range(n_orient)]
        return lax.ppermute(value, ("dom", "orient"), pairs)

    flops = 2 * count * crop * share * width * 2 * lanes
    logits_shape, lse_shape = shape((count, TS, lanes), F32), shape((count, 128), F32)
    slices_shape = shape(slices.shape, F32)
    score_rows, score_columns, back_rows, back_columns = tables

    slots = [particles] + [swap(particles, r) for r in range(1, n_orient)]
    kept = (particles, freq_mask, *tables)
    logits, lse, first, second, bias, mine, mask, *tables = call(
        first_kernel,
        [logits_shape, lse_shape, slices_shape, slices_shape, shape((8, lanes), F32)]
        + [shape(value.shape, value.dtype) for value in kept],
        tuple(
            pltpu.with_memory_space_constraint(value, pltpu.HBM)
            for value in (
                slice_class, slice_orient, class_prior, orient_prior, particles, slices, freq_mask, score_rows,
                score_columns, back_rows, back_columns,
            )
        ),
        [
            pltpu.VMEM(slices.shape, slices.dtype),
            *[pltpu.SMEM(v.shape, v.dtype) for v in (slice_class, slice_orient, class_prior, orient_prior)],
            pltpu.SemaphoreType.DMA((11,)),
        ],
        specs=[hbm] * 11, flops=flops, name="first",
    )
    score_rows, score_columns, back_rows, back_columns = tables
    slots[0] = mine
    scored = [(logits, lse)] + [
        call(
            score_kernel, [logits_shape, lse_shape], (parts, first, second, bias, score_rows, score_columns), [],
            flops=flops, name="score",
        )
        for parts in slots[1:]
    ]
    terms = [[s[1]] for s in scored]
    for b in range(bits(n_orient)):
        sums = [functools.reduce(log_add, t) for t in terms]
        terms = [[sums[r], swap(sums[r ^ (1 << b)], 1 << b)] for r in range(n_orient)]

    rows = crop // block * groups * 8
    steps = bits(n_dom)

    def sent(step, height):
        dtype = BF16
        return shape((height + (8 if dtype == F32 else 16), width), dtype)

    mass_shape = shape((8, lanes), F32)
    turned = pltpu.VMEM((count, crop, width), F32)
    back_scratch = [turned, turned] + [pltpu.VMEM((count * TS, 2 * share * width), BF16)] * 2
    owns, = call(
        functools.partial(own_kernel, share, pack), [shape((count * rows, width), F32)],
        (*scored[0], slots[0], mask, back_rows, back_columns), back_scratch, flops=flops, name="own",
    )
    partial = ()
    for r in range(1, n_orient):
        partial = call(
            functools.partial(back_kernel, share, pack, r == 1, len(terms[r])),
            [shape((rows, width), F32), mass_shape],
            (scored[r][0], slots[r], mask, back_rows, back_columns, *terms[r], *partial),
            back_scratch, flops=flops, name="back",
        )
    keep, send, mass, loglik = call(
        functools.partial(last_back_kernel, share, len(terms[0])),
        [shape((rows // 2, width), F32), sent(0, rows // 2), shape((8, 128), F32), shape((8, 128), F32)],
        (*scored[0], owns, *partial, *terms[0]), [], flops=flops, name="last_back",
    )

    def exchange(value, turned):
        step = turned | parity(turned >> 1, n_dom)
        return lax.ppermute(value, "dom", [(i, i ^ step) for i in range(n_dom)])

    got = exchange(send, 1)
    height = keep.shape[0] // 4
    keep, *sends, mass = call(
        functools.partial(quarter_kernel, groups * 8),
        [shape((height, width), F32)] + [sent(1, height)] * 3 + [shape((8, 128), F32)],
        (keep, got, mass), [], name="quarter",
    )
    gots = [exchange(sends[turn - 1], turn << 1) for turn in (1, 3, 2)]
    for b in range(3, steps):
        height = keep.shape[0] // 2
        keep, send, mass = call(
            functools.partial(halve_kernel, groups * 8, b),
            [shape((height, width), F32), sent(b, height), shape((8, 128), F32)],
            (keep, mass, *gots), [], name="halve",
        )
        gots = [exchange(send, 1 << b)]
    got, = gots
    image, occupancy, loglik = call(
        functools.partial(last_kernel, groups, pack),
        [shape((share, block, width), F32), shape((share,), F32), shape((count,), F32)],
        (keep, got, mass, loglik),
        [
            pltpu.VMEM((share, block, width), F32), pltpu.VMEM((share,), F32), pltpu.VMEM((count,), F32),
            pltpu.SemaphoreType.DMA((3,)),
        ],
        outs_in=hbm, name="last",
    )
    return image, occupancy, loglik


def solution(mesh):
    placed = (P(("dom", "orient"), None, None), P("orient", None, None), P(), P(), P(), P(), P())
    return jax.shard_map(
        functools.partial(shards, mesh.shape["dom"], mesh.shape["orient"]),
        mesh=mesh,
        in_specs=placed,
        out_specs=(P("orient", "dom", None), P("orient"), P(("dom", "orient"))),
        check_vma=False,
    )
```

```python
import functools
import math

import jax
import jax.numpy as jnp
import ml_dtypes
import numpy as np
from jax import lax
from jax.experimental import pallas as pl
from jax.experimental.pallas import tpu as pltpu
from jax.sharding import PartitionSpec as P

TS = 16
F32 = jnp.float32
BF16 = jnp.bfloat16
VMEM_LIMIT = 24 * 1024 * 1024


def phase_tables(crop):
    freq = np.arange(crop, dtype=np.float64) - crop // 2
    offset = np.arange(TS, dtype=np.float64) - TS // 2
    angle = 2.0 * math.pi / crop * freq[:, None] * offset[None, :]
    return np.cos(angle).astype(np.float32), np.sin(angle).astype(np.float32)


def high_low(table):
    high = table.astype(ml_dtypes.bfloat16)
    low = (table - high.astype(np.float32)).astype(ml_dtypes.bfloat16)
    return high, low


def score_tables(crop, share):
    cosine, sine = phase_tables(crop)
    rows = np.zeros((share, 2, crop, 2, share, TS), np.float32)
    for j in range(share):
        rows[j, 0, :, 0, j] = cosine
        rows[j, 0, :, 1, j] = sine
        rows[j, 1, :, 0, j] = -sine
        rows[j, 1, :, 1, j] = cosine
    rows = rows.reshape(share * 2 * crop, 2 * share * TS).astype(ml_dtypes.bfloat16)
    high, low = high_low(np.concatenate([cosine.T, -sine.T], axis=1))
    columns = np.concatenate(
        [np.concatenate([high, high], axis=1), np.concatenate([low, np.zeros_like(low)], axis=1)], axis=0
    )
    return rows, columns


def back_tables(crop, share, order):
    cosine, sine = phase_tables(crop)
    rows = np.zeros((share, TS, 2, share, 2, crop), np.float32)
    for place, j in enumerate(order):
        rows[j, :, 0, place, 0] = cosine.T
        rows[j, :, 0, place, 1] = -sine.T
        rows[j, :, 1, place, 0] = -sine.T
        rows[j, :, 1, place, 1] = -cosine.T
    rows = rows.reshape(share * TS, 2 * share * 2 * crop).astype(ml_dtypes.bfloat16)
    high, low = high_low(np.concatenate([cosine, sine], axis=1))
    return rows, np.concatenate([high, high, low], axis=1)


def score_block(x_ref, first_ref, second_ref, bias, rows_ref, columns_ref, logits_ref, lse_ref):
    count, crop, width = x_ref.shape
    share = first_ref.shape[0]
    lanes = share * TS
    cross = []
    for i in range(count):
        x = x_ref[i].astype(F32)
        turned = pltpu.roll(x, width // 2, 1)
        terms = [(x * first_ref[j] + turned * second_ref[j]).astype(BF16) for j in range(share)]
        cross.append(jnp.concatenate(terms, axis=1))
    rowcorr = jnp.dot(jnp.concatenate(cross, axis=0), rows_ref[...], preferred_element_type=F32)
    high = rowcorr.astype(BF16)
    low = (rowcorr - high.astype(F32)).astype(BF16)
    stacked = jnp.concatenate(
        [
            jnp.concatenate(
                [part[i * crop : (i + 1) * crop, k * lanes : (k + 1) * lanes] for part in (high, low) for k in (0, 1)],
                axis=0,
            )
            for i in range(count)
        ],
        axis=1,
    )
    corr = jnp.dot(columns_ref[...], stacked, preferred_element_type=F32)
    corr = (corr[:TS] + corr[TS:]) * (1.0 / crop)
    logits = [corr[:, i * lanes : (i + 1) * lanes] + bias for i in range(count)]
    for i in range(count):
        logits_ref[i] = logits[i]
    tops = jnp.concatenate([jnp.max(value, axis=0, keepdims=True) for value in logits], axis=0)
    top = jnp.max(tops, axis=1, keepdims=True)
    sums = [jnp.sum(jnp.exp(logits[i] - top[i : i + 1]), axis=0, keepdims=True) for i in range(count)]
    total = jnp.sum(jnp.concatenate(sums, axis=0), axis=1, keepdims=True)
    lse_ref[...] = jnp.broadcast_to(top + jnp.log(total), lse_ref.shape)


def prepare_slices(s_ref, mask_ref, first, second):
    share, crop, width = s_ref.shape
    half = width // 2
    left = lax.broadcasted_iota(jnp.int32, (crop, width), 1) < half
    mask = mask_ref[...].astype(F32)
    mask = jnp.concatenate([mask, mask], axis=1)
    powers = []
    for j in range(share):
        s = s_ref[j].astype(F32) * mask
        turned = pltpu.roll(s, half, 1)
        first[j] = jnp.where(left, s, turned)
        second[j] = jnp.where(left, turned, -s)
        powers.append(jnp.sum(s * s, axis=0, keepdims=True))
    power = jnp.sum(jnp.concatenate(powers, axis=0), axis=1, keepdims=True) * (0.5 / crop)
    slot = lax.broadcasted_iota(jnp.int32, (1, share * TS), 1) // TS
    spread = jnp.zeros((1, share * TS), F32)
    for j in range(share):
        spread = jnp.where(slot == j, power[j : j + 1], spread)
    return spread


def first_kernel(*refs):
    sources, (logits_ref, lse_ref, first, second, bias_ref), kept = refs[:11], refs[11:16], refs[16:22]
    s_ref, class_ref, orient_ref, class_prior_ref, orient_prior_ref, sems = refs[22:]
    x_ref, mask_ref, rows_ref, columns_ref, back_rows_ref, back_columns_ref = kept
    targets = (
        class_ref, orient_ref, class_prior_ref, orient_prior_ref, x_ref, s_ref, mask_ref, rows_ref, columns_ref,
        back_rows_ref, back_columns_ref,
    )
    copies = [pltpu.make_async_copy(a, b, sems.at[k]) for k, (a, b) in enumerate(zip(sources, targets))]
    for copy in copies:
        copy.start()
    share = s_ref.shape[0]
    for copy in copies[:4]:
        copy.wait()
    slot = lax.broadcasted_iota(jnp.int32, (1, share * TS), 1) // TS
    prior = jnp.zeros((1, share * TS), F32)
    start = lax.axis_index("orient") * share
    for j in range(share):
        value = class_prior_ref[class_ref[start + j]] + orient_prior_ref[orient_ref[start + j]]
        prior = jnp.where(slot == j, value, prior)
    for copy in copies[4:7]:
        copy.wait()
    power = prepare_slices(s_ref, mask_ref, first, second)
    for copy in copies[7:9]:
        copy.wait()
    bias = prior - power
    bias_ref[...] = jnp.broadcast_to(bias, bias_ref.shape)
    score_block(x_ref, first, second, bias, rows_ref, columns_ref, logits_ref, lse_ref)
    for copy in copies[9:]:
        copy.wait()


def score_kernel(x_ref, first, second, bias_ref, rows_ref, columns_ref, logits_ref, lse_ref):
    score_block(x_ref, first, second, bias_ref[:1], rows_ref, columns_ref, logits_ref, lse_ref)


def log_add(a, b):
    top = jnp.maximum(a, b)
    return top + jnp.log(jnp.exp(a - top) + jnp.exp(b - top))


def parity(index, limit):
    total = index & 1
    for b in range(1, bits(limit)):
        total = total ^ ((index >> b) & 1)
    return total


def to_lanes(column):
    wide = jnp.broadcast_to(column, (column.shape[0], 128))
    row = lax.broadcasted_iota(jnp.int32, wide.shape, 0)
    lane = lax.broadcasted_iota(jnp.int32, wide.shape, 1)
    return jnp.sum(jnp.where(row == lane, wide, 0.0), axis=0, keepdims=True)


def put_mass(send_ref, at, mass):
    row = lax.broadcasted_iota(jnp.int32, (8, 128), 0)
    if send_ref.dtype == F32:
        send_ref[at : at + 8] = jnp.broadcast_to(mass, (8, 128))
    else:
        high = mass.astype(BF16).astype(F32)
        middle = (mass - high).astype(BF16).astype(F32)
        low = mass - high - middle
        terms = jnp.where(row == 0, high, jnp.where(row == 1, middle, jnp.where(row == 2, low, 0.0)))
        send_ref[at : at + 16] = jnp.concatenate([terms, jnp.zeros((8, 128), F32)], axis=0).astype(BF16)


def get_mass(got_ref, at):
    if got_ref.dtype == F32:
        return got_ref[at : at + 1]
    terms = got_ref[at : at + 16].astype(F32)
    return terms[0:1] + terms[1:2] + terms[2:3]


def double_particles(x_ref, doubled_re, doubled_im):
    count, crop, width = x_ref.shape
    left = lax.broadcasted_iota(jnp.int32, (crop, width), 1) < width // 2
    for i in range(count):
        x = x_ref[i].astype(F32)
        turned = pltpu.roll(x, width // 2, 1)
        doubled_re[i] = jnp.where(left, x, turned)
        doubled_im[i] = jnp.where(left, turned, x)


def put_spread(spread, high, low):
    rounded = spread.astype(BF16)
    high[...] = rounded
    low[...] = (spread - rounded.astype(F32)).astype(BF16)


def kernel_of(high, low, columns, k, group, wide):
    rows = slice(k * TS, (k + 1) * TS)
    here = slice(group * wide, (group + 1) * wide)
    there = slice(high.shape[1] // 2 + group * wide, high.shape[1] // 2 + (group + 1) * wide)
    a, b = high[rows, here], high[rows, there]
    terms = jnp.concatenate([a, b, low[rows, here], low[rows, there], a, b], axis=0)
    return jnp.dot(columns, terms, preferred_element_type=F32)


def put_images(re, im, mask, odd, pack, group, groups, out_ref, at):
    crop, width = mask.shape
    half = width // 2
    signed = jnp.where(lax.broadcasted_iota(jnp.int32, (1, width), 1) < half, -mask, mask)
    images = []
    for p in range(pack):
        here = slice(p * width, (p + 1) * width)
        images.append(re[:, here] * mask + pltpu.roll(im[:, here], half, 1) * signed)
    block = 8 // pack
    tiles = [jnp.concatenate([image[r : r + block] for image in images], axis=0) for r in range(0, crop, block)]
    pairs = len(tiles) // 2
    for pair in range(pairs):
        even, other = tiles[2 * pair], tiles[2 * pair + 1]
        if parity(pair, crop):
            even, other = other, even
        kept, given = at + (pair * groups + group) * 8, at + ((pairs + pair) * groups + group) * 8
        out_ref[kept : kept + 8] = jnp.where(odd == 1, other, even)
        out_ref[given : given + 8] = jnp.where(odd == 1, even, other)


def twice_mask(mask_ref):
    mask = mask_ref[...].astype(F32)
    return jnp.concatenate([mask, mask], axis=1)


def own_kernel(
    share, pack, logits_ref, lse_ref, x_ref, mask_ref, rows_ref, columns_ref, out_ref, doubled_re, doubled_im, high, low
):
    count, crop, width = x_ref.shape
    double_particles(x_ref, doubled_re, doubled_im)
    weights = jnp.concatenate([jnp.exp(logits_ref[i] - lse_ref[i : i + 1, :]) for i in range(count)], axis=0)
    rounded = weights.astype(BF16)
    rest = (weights - rounded.astype(F32)).astype(BF16)
    rows = rows_ref[...]
    put_spread(
        jnp.dot(rounded, rows, preferred_element_type=F32) + jnp.dot(rest, rows, preferred_element_type=F32), high, low
    )
    columns = columns_ref[...]
    mask = twice_mask(mask_ref)
    odd = parity(lax.axis_index("dom"), crop * pack // 8)
    height = crop * share
    for group in range(share // pack):
        for k in range(count):
            kernel = kernel_of(high, low, columns, k, group, pack * width)
            re = kernel * jnp.concatenate([doubled_re[k]] * pack, axis=1)
            im = kernel * jnp.concatenate([doubled_im[k]] * pack, axis=1)
            put_images(re, im, mask, odd, pack, group, share // pack, out_ref, k * height)


def back_kernel(share, pack, start, n_lse, *refs):
    refs = list(refs)
    logits_ref, x_ref, mask_ref, rows_ref, columns_ref = refs[:5]
    lse_refs = refs[5 : 5 + n_lse]
    del refs[: 5 + n_lse]
    if not start:
        out_in, mass_in = refs[:2]
        del refs[:2]
    out_ref, mass_ref, doubled_re, doubled_im, high, low = refs
    count, crop, width = x_ref.shape
    loglik = functools.reduce(log_add, [ref[...] for ref in lse_refs])
    double_particles(x_ref, doubled_re, doubled_im)
    mass = jnp.zeros((TS, share * TS), F32)
    weights = []
    for i in range(count):
        weight = jnp.exp(logits_ref[i] - loglik[i : i + 1, :]).astype(BF16)
        mass = mass + weight.astype(F32)
        weights.append(weight)
    mass = jnp.sum(mass, axis=0, keepdims=True)
    if not start:
        mass = mass + mass_in[:1]
    mass_ref[...] = jnp.broadcast_to(mass, mass_ref.shape)
    put_spread(jnp.dot(jnp.concatenate(weights, axis=0), rows_ref[...], preferred_element_type=F32), high, low)
    wide = pack * width
    columns = columns_ref[...]
    mask = twice_mask(mask_ref)
    odd = parity(lax.axis_index("dom"), crop * pack // 8)
    for group in range(share // pack):
        re = jnp.zeros((crop, wide), F32)
        im = jnp.zeros((crop, wide), F32)
        for k in range(count):
            kernel = kernel_of(high, low, columns, k, group, wide)
            re = re + kernel * jnp.concatenate([doubled_re[k]] * pack, axis=1)
            im = im + kernel * jnp.concatenate([doubled_im[k]] * pack, axis=1)
        put_images(re, im, mask, odd, pack, group, share // pack, out_ref, 0)
    if not start:
        out_ref[...] = out_ref[...] + out_in[...]


def last_back_kernel(share, n_lse, logits_ref, lse_ref, own_ref, sum_ref, mass_in, *refs):
    lse_refs = refs[:n_lse]
    keep_ref, send_ref, mass_ref, loglik_ref = refs[n_lse:]
    count = logits_ref.shape[0]
    loglik = functools.reduce(log_add, [ref[...] for ref in lse_refs])
    factor = jnp.exp(lse_ref[...] - loglik)
    mass = jnp.zeros((TS, share * TS), F32)
    for i in range(count):
        mass = mass + jnp.exp(logits_ref[i] - loglik[i : i + 1, :]).astype(BF16).astype(F32)
    mass = jnp.sum(mass, axis=0, keepdims=True) + mass_in[:1]
    row = lax.broadcasted_iota(jnp.int32, (share, share * TS), 0)
    lane = lax.broadcasted_iota(jnp.int32, (share, share * TS), 1)
    mass = to_lanes(jnp.sum(jnp.where(row == lane // TS, mass, 0.0), axis=1, keepdims=True))
    height = sum_ref.shape[0]
    half = height // 2
    factors = [jnp.broadcast_to(factor[i : i + 1, :], (8, factor.shape[1])) for i in range(count)]
    for at in range(0, height, 8):
        total = sum_ref[at : at + 8]
        for i in range(count):
            total = total + own_ref[i * height + at : i * height + at + 8] * factors[i]
        if at < half:
            keep_ref[at : at + 8] = total
        else:
            send_ref[at - half : at - half + 8] = total
    put_mass(send_ref, half, mass)
    loglik_ref[...] = jnp.broadcast_to(to_lanes(loglik[:, :1]), loglik_ref.shape)
    mass_ref[...] = jnp.broadcast_to(mass, mass_ref.shape)


def quarter_kernel(unit, keep_ref, got_ref, mass_in, left_ref, *refs):
    sends, mass_ref = refs[:-1], refs[-1]
    rows = keep_ref.shape[0]
    own = (lax.axis_index("dom") >> 1) & 3
    mass = mass_in[:1] + get_mass(got_ref, rows)
    for turn, out_ref in enumerate((left_ref, *sends)):
        for rest in range(rows // unit // 4):
            at = rest * unit
            here = pl.ds(pl.multiple_of((4 * rest + (own ^ turn)) * unit, unit), unit)
            out_ref[at : at + unit] = (keep_ref[here] + got_ref[here].astype(F32)).astype(out_ref.dtype)
        if turn:
            put_mass(out_ref, rows // 4, mass)
    mass_ref[...] = jnp.broadcast_to(mass, mass_ref.shape)


def halve_kernel(unit, bit, keep_ref, mass_in, *refs):
    gots, (left_ref, send_ref, mass_ref) = refs[:-3], refs[-3:]
    rows = keep_ref.shape[0]
    side = (lax.axis_index("dom") >> bit) & 1
    mass = mass_in[:1]
    for got_ref in gots:
        mass = mass + get_mass(got_ref, rows)
    for pair in range(rows // unit // 2):
        at = pair * unit
        for half, out_ref in ((side, left_ref), (1 - side, send_ref)):
            here = pl.ds(pl.multiple_of((2 * pair + half) * unit, unit), unit)
            total = keep_ref[here]
            for got_ref in gots:
                total = total + got_ref[here].astype(F32)
            out_ref[at : at + unit] = total.astype(out_ref.dtype)
    put_mass(send_ref, rows // 2, mass)
    mass_ref[...] = jnp.broadcast_to(mass, mass_ref.shape)


def last_kernel(
    groups, pack, keep_ref, got_ref, mass_in, loglik_in, image_out, occupancy_out, loglik_out,
    image_ref, occupancy_ref, loglik_ref, sems,
):
    loglik_ref[...] = loglik_in[0, : loglik_ref.shape[0]]
    copies = [pltpu.make_async_copy(loglik_ref, loglik_out, sems.at[0])]
    copies[0].start()
    block = image_ref.shape[1]
    rows = keep_ref.shape[0]
    total = keep_ref[...] + got_ref[:rows].astype(F32)
    for g in range(groups):
        for p in range(pack):
            image_ref[p * groups + g] = total[g * 8 + p * block : g * 8 + (p + 1) * block]
    copies.append(pltpu.make_async_copy(image_ref, image_out, sems.at[1]))
    copies[1].start()
    mass = mass_in[:1] + get_mass(got_ref, rows)
    occupancy_ref[...] = mass[0, : occupancy_ref.shape[0]]
    copies.append(pltpu.make_async_copy(occupancy_ref, occupancy_out, sems.at[2]))
    copies[2].start()
    for copy in copies:
        copy.wait()


def bits(count):
    return count.bit_length() - 1


def shards(n_dom, n_orient, particles, slices, freq_mask, slice_class, slice_orient, class_prior, orient_prior):
    count, crop, width = particles.shape
    share = slices.shape[0]
    lanes = share * TS
    block = crop // n_dom
    pack = 8 // block
    groups = share // pack
    vmem = pl.BlockSpec(memory_space=pltpu.VMEM)
    hbm = pl.BlockSpec(memory_space=pltpu.HBM)
    shape = jax.ShapeDtypeStruct
    params = pltpu.CompilerParams(vmem_limit_bytes=VMEM_LIMIT)
    order = [p * groups + g for g in range(groups) for p in range(pack)]
    tables = [jnp.asarray(t) for t in (*score_tables(crop, share), *back_tables(crop, share, order))]

    def call(kernel, outs, args, scratch, specs=None, outs_in=vmem, flops=0, name=None):
        return pl.pallas_call(
            kernel,
            out_shape=tuple(outs),
            in_specs=specs or [vmem] * len(args),
            out_specs=(outs_in,) * len(outs),
            scratch_shapes=scratch,
            compiler_params=params,
            cost_estimate=pl.CostEstimate(flops=flops, bytes_accessed=1 << 20, transcendentals=0),
            name=name,
        )(*args)

    def swap(value, r):
        core = parity(r, n_orient)
        pairs = [(d * n_orient + o, (d ^ core) * n_orient + (o ^ r)) for d in range(n_dom) for o in range(n_orient)]
        return lax.ppermute(value, ("dom", "orient"), pairs)

    flops = 2 * count * crop * share * width * 2 * lanes
    logits_shape, lse_shape = shape((count, TS, lanes), F32), shape((count, 128), F32)
    slices_shape = shape(slices.shape, F32)
    score_rows, score_columns, back_rows, back_columns = tables

    slots = [particles] + [swap(particles, r) for r in range(1, n_orient)]
    kept = (particles, freq_mask, *tables)
    logits, lse, first, second, bias, mine, mask, *tables = call(
        first_kernel,
        [logits_shape, lse_shape, slices_shape, slices_shape, shape((8, lanes), F32)]
        + [shape(value.shape, value.dtype) for value in kept],
        tuple(
            pltpu.with_memory_space_constraint(value, pltpu.HBM)
            for value in (
                slice_class, slice_orient, class_prior, orient_prior, particles, slices, freq_mask, score_rows,
                score_columns, back_rows, back_columns,
            )
        ),
        [
            pltpu.VMEM(slices.shape, slices.dtype),
            *[pltpu.SMEM(v.shape, v.dtype) for v in (slice_class, slice_orient, class_prior, orient_prior)],
            pltpu.SemaphoreType.DMA((11,)),
        ],
        specs=[hbm] * 11, flops=flops, name="first",
    )
    score_rows, score_columns, back_rows, back_columns = tables
    slots[0] = mine
    scored = [(logits, lse)] + [
        call(
            score_kernel, [logits_shape, lse_shape], (parts, first, second, bias, score_rows, score_columns), [],
            flops=flops, name="score",
        )
        for parts in slots[1:]
    ]
    terms = [[s[1]] for s in scored]
    for b in range(bits(n_orient)):
        sums = [functools.reduce(log_add, t) for t in terms]
        terms = [[sums[r], swap(sums[r ^ (1 << b)], 1 << b)] for r in range(n_orient)]

    rows = crop // block * groups * 8
    steps = bits(n_dom)

    def sent(step, height):
        dtype = F32 if step in (0, steps - 1) else BF16
        return shape((height + (8 if dtype == F32 else 16), width), dtype)

    mass_shape = shape((8, lanes), F32)
    turned = pltpu.VMEM((count, crop, width), F32)
    back_scratch = [turned, turned] + [pltpu.VMEM((count * TS, 2 * share * width), BF16)] * 2
    owns, = call(
        functools.partial(own_kernel, share, pack), [shape((count * rows, width), F32)],
        (*scored[0], slots[0], mask, back_rows, back_columns), back_scratch, flops=flops, name="own",
    )
    partial = ()
    for r in range(1, n_orient):
        partial = call(
            functools.partial(back_kernel, share, pack, r == 1, len(terms[r])),
            [shape((rows, width), F32), mass_shape],
            (scored[r][0], slots[r], mask, back_rows, back_columns, *terms[r], *partial),
            back_scratch, flops=flops, name="back",
        )
    keep, send, mass, loglik = call(
        functools.partial(last_back_kernel, share, len(terms[0])),
        [shape((rows // 2, width), F32), sent(0, rows // 2), shape((8, 128), F32), shape((8, 128), F32)],
        (*scored[0], owns, *partial, *terms[0]), [], flops=flops, name="last_back",
    )

    def exchange(value, turned):
        step = turned | parity(turned >> 1, n_dom)
        return lax.ppermute(value, "dom", [(i, i ^ step) for i in range(n_dom)])

    got = exchange(send, 1)
    height = keep.shape[0] // 4
    keep, *sends, mass = call(
        functools.partial(quarter_kernel, groups * 8),
        [shape((height, width), F32)] + [sent(1, height)] * 3 + [shape((8, 128), F32)],
        (keep, got, mass), [], name="quarter",
    )
    gots = [exchange(sends[turn - 1], turn << 1) for turn in (3, 2, 1)]
    for b in range(3, steps):
        height = keep.shape[0] // 2
        keep, send, mass = call(
            functools.partial(halve_kernel, groups * 8, b),
            [shape((height, width), F32), sent(b, height), shape((8, 128), F32)],
            (keep, mass, *gots), [], name="halve",
        )
        gots = [exchange(send, 1 << b)]
    got, = gots
    image, occupancy, loglik = call(
        functools.partial(last_kernel, groups, pack),
        [shape((share, block, width), F32), shape((share,), F32), shape((count,), F32)],
        (keep, got, mass, loglik),
        [
            pltpu.VMEM((share, block, width), F32), pltpu.VMEM((share,), F32), pltpu.VMEM((count,), F32),
            pltpu.SemaphoreType.DMA((3,)),
        ],
        outs_in=hbm, name="last",
    )
    return image, occupancy, loglik


def solution(mesh):
    placed = (P(("dom", "orient"), None, None), P("orient", None, None), P(), P(), P(), P(), P())
    return jax.shard_map(
        functools.partial(shards, mesh.shape["dom"], mesh.shape["orient"]),
        mesh=mesh,
        in_specs=placed,
        out_specs=(P("orient", "dom", None), P("orient"), P(("dom", "orient"))),
        check_vma=False,
    )
```
